512 devices in a mesh: label: 64 (over y, z), cent: 8 (over x, core).
Axes of the slice: x: 4, y: 4, z: 16, core: 2. Of those that a mesh axis runs over, the one named last changes fastest.
Arguments:
- labels: bfloat16 [32768, 256], P('label'), may hold values from -6 to 6
- counts: int32 [64], P('label'), may hold values from 1 to 512, 16384 in all
- centroids: bfloat16 [32768, 256], P('cent'), may hold values from -6 to 6
Outputs:
- new_centroids: float32 [32768, 256], P(('cent', 'label'))
- code_mass: float32 [32768], P('cent')
The draws below stay inside these ranges and needn't reach their ends.
Inputs may be any that keep to these rules, and one draw needn't show every extreme that they name: Label device i holds its live rows in its first counts[i] slots, the rest are padding; the counts sum to 16384 and at least one device has all 512 slots live.
All inputs are finite; a program needn't handle non-finite values.
Results may differ from the reference program's by a relative error of at most 0.0072.
Values sent between devices are 32-bit elements; how exact they have to be, the bound alone decides.
A program may use at most 64 MiB of HBM per device.

```python
import math
import jax
import jax.numpy as jnp
import numpy as np
from jax import lax

EMBED_WIDTH = 256
KC = 4096
LAB_DEV = 512
ITERS = 3
K = 32768
SLOTS = 32768
LIVE = 16384
N_LABEL = 64
N_CENT = 8


def shard_levels(stream_key, extent, pieces, least, high):
    factor_of = 1.0
    for dim, parts in pieces:
        draws = jax.random.uniform(jax.random.fold_in(jax.random.fold_in(stream_key, 6), dim), (parts,), jnp.float32, least / len(pieces), high / len(pieces))
        factor_of = factor_of * jnp.repeat(jnp.exp(draws), extent[dim] // parts).reshape((-1,) + (1,) * (len(extent) - 1 - dim))
    return factor_of


def profile(number_of, total, limit, skew):
    portions = [(1 << 20) // math.isqrt(rank ** skew) + 1 for rank in range(2, number_of + 1)]
    surplus, given = total - limit - (number_of - 1), [1] * (number_of - 1)
    while surplus > 0:
        movable = [i for i in range(number_of - 1) if given[i] < limit]
        mass, left = sum([portions[i] for i in movable]), surplus
        for i in movable:
            addition = min(limit - given[i], max(1, left * portions[i] // mass), surplus)
            given[i] = given[i] + addition
            surplus = surplus - addition
    return np.array([limit] + given)


def ragged_sizes(own_key, number_of, total, most, lean):
    if number_of == 2:
        one = jax.random.randint(own_key, (), max(1, total - most), min(most, total - 1) + 1)
        return jnp.stack([one, total - one])
    tallies = jnp.asarray(profile(number_of, total, most, lean), jnp.int32)
    couples = (number_of - 1) // 2
    donor, sink = tallies[1:1 + 2 * couples:2], tallies[2:2 + 2 * couples:2]
    room = jnp.minimum(donor - 1, most - sink)
    shifted = jax.random.randint(jax.random.fold_in(own_key, 1), (couples,), 0, 1 << 20) % (room + 1)
    tallies = tallies.at[1:1 + 2 * couples:2].set(donor - shifted).at[2:2 + 2 * couples:2].set(sink + shifted)
    return tallies[jax.random.permutation(jax.random.fold_in(own_key, 2), number_of)]


def gaussian(rng, extent, scale, reach, pieces=(), held_as=jnp.bfloat16):
    entries = scale * jax.random.normal(rng, extent, jnp.float32)
    if pieces:
        entries = entries * shard_levels(rng, extent, pieces, -0.22, 0.18)
    return jnp.clip(entries, -reach, reach).astype(held_as)


def setup_inputs(seed: int = 0) -> dict:
    key_list = jax.random.split(jax.random.key(seed), 4)
    labels = gaussian(key_list[0], (SLOTS, EMBED_WIDTH), 1.0, 6.0, ((0, 64),))
    counts = ragged_sizes(key_list[1], N_LABEL, LIVE, LAB_DEV, 2).astype(jnp.int32)
    centroids = gaussian(key_list[2], (K, EMBED_WIDTH), 1.0, 6.0, ((0, 8),))
    return {"labels": labels, "counts": counts, "centroids": centroids}


SOFTMAX_HEAT = 0.02
EPSILON = 1e-06

def unit_rows(input_values):
    widened = input_values.astype(jnp.float32)
    scale = lax.rsqrt(lax.optimization_barrier(jnp.mean(widened * widened, axis=1, keepdims=True)) + EPSILON)
    return (widened * scale).astype(jnp.bfloat16)

def reference(labels, counts, centroids):
    slot_index = jnp.arange(SLOTS, dtype=jnp.int32)
    owner = slot_index // LAB_DEV
    live_mask = slot_index - owner * LAB_DEV < counts[owner]
    chosen = jnp.nonzero(live_mask, size=LIVE)[0].astype(jnp.int32)
    label_unit = unit_rows(labels)[chosen]
    centroid_unit = unit_rows(centroids)
    blocks = centroid_unit.reshape(N_CENT, KC, EMBED_WIDTH)

    def kernel_block(block):
        affinity_scores = lax.dot_general(label_unit, block, (((1,), (1,)), ((), ())), preferred_element_type=jnp.float32)
        return jnp.exp(affinity_scores * (1.0 / (SOFTMAX_HEAT * EMBED_WIDTH))).astype(jnp.bfloat16)

    def column_sums(row_scale):

        def one_block(block):
            return jnp.dot(row_scale, kernel_block(block), preferred_element_type=jnp.float32, precision=lax.Precision.HIGHEST)
        return lax.map(one_block, blocks).reshape(K)

    def row_sums(col_scale):
        scale_blocks = col_scale.reshape(N_CENT, KC)

        def add_block(carried, pair):
            block, scale_part = pair
            return (carried + jnp.dot(kernel_block(block), scale_part, preferred_element_type=jnp.float32, precision=lax.Precision.HIGHEST), None)
        summed, _ = lax.scan(add_block, jnp.zeros((LIVE,), jnp.float32), (blocks, scale_blocks))
        return summed
    row_scale = jnp.ones((LIVE,), jnp.float32)
    col_scale = jnp.ones((K,), jnp.float32)
    for iteration in range(ITERS):
        col_scale = 1.0 / column_sums(row_scale)
        row_scale = 1.0 / row_sums(col_scale)
    code_mass = col_scale * column_sums(row_scale)

    def stat_block(block):
        plan_weights = (row_scale[:, None] * kernel_block(block)).astype(jnp.bfloat16)
        return lax.dot_general(plan_weights, label_unit, (((0,), (0,)), ((), ())), preferred_element_type=jnp.float32)
    stats = lax.map(stat_block, blocks).reshape(K, EMBED_WIDTH)
    new_centroids = stats * lax.rsqrt(lax.optimization_barrier(jnp.mean(stats * stats, axis=1, keepdims=True)) + EPSILON)
    return (new_centroids, code_mass)
```

```python
import functools

import jax
import jax.numpy as jnp
from jax import lax
from jax.experimental import pallas as pl
from jax.experimental.pallas import tpu as pltpu
from jax.sharding import PartitionSpec as P

ITERS = 3
SOFTMAX_HEAT = 0.02
EPSILON = 1e-06

F32, BF16 = jnp.float32, jnp.bfloat16
MESH = pl.DeviceIdType.MESH
NT = (((1,), (1,)), ((), ()))

NY, NZ, NX, NK = 4, 16, 4, 2
LAB = 512
HALF = LAB // 2
WIDE = NY * LAB
KC = 4096
QUARTER = KC // NY
SIDE = WIDE // 2
FEAT = 256
BLOCK = QUARTER // NZ
TILE = 256
EXTRA = 8
CHUNKS = 2
PIECE = BLOCK // CHUNKS


def distance(offset, size):
    return min(offset, size - offset)


Y_OFFSETS = (2, 1, 3)
Z_OFFSETS = sorted(range(1, NZ), key=lambda d: -distance(d, NZ))
XY_OFFSETS = sorted(
    [(dy, dx) for dy in range(NY) for dx in range(NX) if dy or dx],
    key=lambda o: -(distance(o[0], NY) + distance(o[1], NX)),
)


def unit(values):
    wide = values.astype(F32)
    scale = lax.rsqrt(jnp.mean(wide * wide, axis=1, keepdims=True) + EPSILON)
    return (wide * scale).astype(BF16)


def gibbs(centroid_unit, label_unit):
    scores = lax.dot_general(centroid_unit, label_unit, NT, preferred_element_type=F32)
    return jnp.exp(scores * (1.0 / (SOFTMAX_HEAT * FEAT))).astype(BF16)


def split_rows(vector):
    high = vector.astype(BF16).astype(F32)
    rest = vector - high
    row = lax.broadcasted_iota(jnp.int32, (16, vector.shape[1]), 0)
    return jnp.where(row == 0, high, jnp.where(row == 1, rest, 0.0)).astype(BF16)


def joined(rows):
    return rows[0:1, :] + rows[1:2, :]


def kernel(
    counts_ref,
    lab_ref,
    cen_ref,
    new_ref,
    mass_ref,
    cen_unit,
    wide_gibbs,
    gibbs_t,
    lab_all,
    lab_send,
    lab_land,
    mask_all,
    row_scale,
    first_src,
    first_land,
    z_src,
    z_land,
    core_src,
    core_land,
    xy_src,
    xy_land,
    half_src,
    half_land,
    mass_src,
    mass_land,
    right_src,
    right_land,
    left_src,
    left_land,
    s_first, r_first,
    s_lab, r_lab,
    s_fwd, r_fwd,
    s_z, r_z,
    s_core, r_core,
    s_xy, r_xy,
    s_half, r_half,
    s_mass, r_mass,
    s_right, r_right,
    s_left, r_left,
):
    label, cent = lax.axis_index("label"), lax.axis_index("cent")
    y, z = label // NZ, lax.rem(label, NZ)
    x, k = cent // NK, lax.rem(cent, NK)
    other = 1 - k

    def at(dy=0, dz=0, dx=0):
        return (
            lax.rem(y + dy, NY) * NZ + lax.rem(z + dz, NZ),
            lax.rem(x + dx, NX) * NK + k,
        )

    partner = (label, x * NK + other)

    def send(src, dst, send_sem, recv_sem, device):
        pltpu.make_async_remote_copy(
            src_ref=src,
            dst_ref=dst,
            send_sem=send_sem,
            recv_sem=recv_sem,
            device_id=device,
            device_id_type=MESH,
        ).start()

    def arrived(dst, send_sem, recv_sem):
        pltpu.make_async_remote_copy(
            src_ref=dst,
            dst_ref=dst,
            send_sem=send_sem,
            recv_sem=recv_sem,
            device_id=partner,
            device_id_type=MESH,
        ).wait_recv()

    def sent(src, send_sem, recv_sem):
        pltpu.make_async_remote_copy(
            src_ref=src,
            dst_ref=src,
            send_sem=send_sem,
            recv_sem=recv_sem,
            device_id=partner,
            device_id_type=MESH,
        ).wait_send()

    barrier = pltpu.get_barrier_semaphore()
    for dz in Z_OFFSETS:
        pl.semaphore_signal(barrier, inc=1, device_id=at(dz=dz), device_id_type=MESH)
    for dy, dx in XY_OFFSETS:
        pl.semaphore_signal(
            barrier, inc=1, device_id=at(dy=dy, dx=dx), device_id_type=MESH
        )
    pl.semaphore_signal(barrier, inc=1, device_id=partner, device_id_type=MESH)

    count = counts_ref[0]
    own_rows = pl.multiple_of(y * LAB, LAB)
    for half in range(2):
        rows = slice(half * HALF, (half + 1) * HALF)
        unit_half = unit(lab_ref[rows, :])
        lab_all[pl.ds(own_rows + half * HALF, HALF), :] = unit_half
        lab_send[half, 0:HALF, :] = unit_half.astype(F32)
        slot = lax.broadcasted_iota(jnp.int32, (EXTRA, HALF), 1) + half * HALF
        lab_send[half, HALF : HALF + EXTRA, :] = jnp.where(slot < count, 1.0, 0.0)
    slot = lax.broadcasted_iota(jnp.int32, (16, LAB), 1)
    own_mask = jnp.where(slot < count, 1.0, 0.0)
    mask_all[:, pl.ds(own_rows, LAB)] = own_mask[0:1, :]
    own_mask = own_mask.astype(BF16)
    own_unit = lab_all[pl.ds(own_rows, LAB), :]

    for part in range(NY):
        def first_tile(j, _, part=part):
            rows = pl.ds(pl.multiple_of(part * QUARTER + j * TILE, TILE), TILE)
            tile_unit = unit(cen_ref[rows, :])
            cen_unit[rows, :] = tile_unit
            tile = gibbs(tile_unit, own_unit)
            wide_gibbs[rows, :] = tile
            sums = lax.dot_general(own_mask, tile, NT, preferred_element_type=F32)
            first_src[part, :, pl.ds(pl.multiple_of(j * TILE, TILE), TILE)] = sums[0:1, :]
            return 0

        lax.fori_loop(0, QUARTER // TILE, first_tile, 0)

    pl.semaphore_wait(barrier, NZ - 1 + NY * NX - 1 + 1)

    for dy in Y_OFFSETS:
        send(
            first_src.at[lax.rem(y + dy, NY)], first_land.at[dy - 1],
            s_first, r_first, at(dy=dy),
        )
    for dy in Y_OFFSETS:
        send(
            lab_send.at[k], lab_land.at[dy - 1, k],
            s_lab, r_lab.at[dy - 1], at(dy=dy),
        )

    def own_quarter(j, _):
        rows = pl.ds(pl.multiple_of(j * TILE, TILE), TILE)
        mine = pl.ds(pl.multiple_of(y * QUARTER + j * TILE, TILE), TILE)
        gibbs_t[rows, pl.ds(own_rows, LAB)] = wide_gibbs[mine, :]
        return 0

    lax.fori_loop(0, QUARTER // TILE, own_quarter, 0)

    def z_send(turn):
        for dz in Z_OFFSETS:
            send(z_src.at[turn], z_land.at[turn, dz - 1], s_z.at[turn], r_z.at[turn], at(dz=dz))

    def z_total(turn):
        arrived(z_land.at[turn], s_z.at[turn], r_z.at[turn])
        total = z_src[turn]
        for slot in range(NZ - 1):
            total = total + z_land[turn, slot]
        return total

    arrived(first_land, s_first, r_first)
    z_src[0] = first_src[y] + first_land[0] + first_land[1] + first_land[2]
    z_send(0)

    def take(dy, half):
        owner = lax.rem(y + (NY - dy), NY)
        rows = pl.ds(pl.multiple_of(owner * LAB + half * HALF, HALF), HALF)
        landed = lab_land[dy - 1, half, 0:HALF, :].astype(BF16)
        lab_all[rows, :] = landed
        mask_all[:, rows] = lab_land[dy - 1, half, HALF : HALF + 1, :]

        def tile(j, _):
            out = pl.ds(pl.multiple_of(j * TILE, TILE), TILE)
            mine = pl.ds(pl.multiple_of(y * QUARTER + j * TILE, TILE), TILE)
            gibbs_t[out, rows] = gibbs(cen_unit[mine, :], landed)
            return 0

        lax.fori_loop(0, QUARTER // TILE, tile, 0)

    for dy in (1, 3, 2):
        arrived(lab_land.at[dy - 1, k], s_lab, r_lab.at[dy - 1])
        send(
            lab_land.at[dy - 1, k], lab_land.at[dy - 1, k],
            s_fwd, r_fwd.at[dy - 1], partner,
        )
        take(dy, k)
    for dy in (1, 3, 2):
        arrived(lab_land.at[dy - 1, other], s_fwd, r_fwd.at[dy - 1])
        take(dy, other)

    def row_stage(turn, col_scale):
        scale_rows = split_rows(col_scale)
        for half in range(2):
            columns = slice(half * SIDE, (half + 1) * SIDE)
            core_src[turn, half] = joined(
                jnp.dot(scale_rows, gibbs_t[:, columns], preferred_element_type=F32)
            )
        send(core_src.at[turn, other], core_land.at[turn], s_core.at[turn], r_core.at[turn], partner)
        arrived(core_land.at[turn], s_core.at[turn], r_core.at[turn])
        xy_src[turn] = core_src[turn, k] + core_land[turn]
        for dy, dx in XY_OFFSETS:
            send(
                xy_src.at[turn], xy_land.at[turn, dy * NX + dx - 1],
                s_xy.at[turn], r_xy.at[turn], at(dy=dy, dx=dx),
            )
        arrived(xy_land.at[turn], s_xy.at[turn], r_xy.at[turn])
        total = xy_src[turn]
        for slot in range(NY * NX - 1):
            total = total + xy_land[turn, slot]
        mine = pl.ds(pl.multiple_of(k * SIDE, SIDE), SIDE)
        scale = mask_all[:, mine] / total
        half_src[turn] = scale
        send(half_src.at[turn], half_land.at[turn], s_half.at[turn], r_half.at[turn], partner)
        row_scale[:, mine] = scale
        arrived(half_land.at[turn], s_half.at[turn], r_half.at[turn])
        row_scale[:, pl.ds(pl.multiple_of(other * SIDE, SIDE), SIDE)] = half_land[turn]

    def col_stage(turn):
        scale_rows = split_rows(row_scale[...])
        for j in range(QUARTER // TILE):
            rows = slice(j * TILE, (j + 1) * TILE)
            z_src[turn, :, rows] = joined(
                lax.dot_general(scale_rows, gibbs_t[rows, :], NT, preferred_element_type=F32)
            )
        z_send(turn)

    col_scale = 1.0 / z_total(0)
    for turn in range(ITERS):
        if turn:
            col_stage(turn)
            col_scale = 1.0 / z_total(turn)
        row_stage(turn, col_scale)

    def block_stats(owner):
        rows = pl.ds(pl.multiple_of(owner * BLOCK, BLOCK), BLOCK)
        weights = (gibbs_t[rows, :].astype(F32) * row_scale[...]).astype(BF16)
        return jnp.dot(weights, lab_all[...], preferred_element_type=F32)

    to_right, to_left = at(dz=1), at(dz=NZ - 1)

    def pass_on(step, piece, src, land, s_sem, r_sem, device):
        send(src.at[step, piece], land.at[step, piece], s_sem, r_sem.at[step, piece], device)

    right = block_stats(lax.rem(z + 8, NZ))
    for piece in range(CHUNKS):
        right_src[0, piece] = right[piece * PIECE : (piece + 1) * PIECE, :]
        pass_on(0, piece, right_src, right_land, s_right, r_right, to_right)
    left = block_stats(lax.rem(z + NZ - 7, NZ))
    for piece in range(CHUNKS):
        left_src[0, piece] = left[piece * PIECE : (piece + 1) * PIECE, :]
        pass_on(0, piece, left_src, left_land, s_left, r_left, to_left)

    col_stage(ITERS)

    def ring_step(step, _):
        right = block_stats(lax.rem(z + 8 - step, NZ))
        left = block_stats(lax.rem(z + NZ - 7 + step, NZ))
        for piece in range(CHUNKS):
            part = slice(piece * PIECE, (piece + 1) * PIECE)
            arrived(right_land.at[step - 1, piece], s_right, r_right.at[step - 1, piece])
            right_src[step, piece] = right[part, :] + right_land[step - 1, piece]
            pass_on(step, piece, right_src, right_land, s_right, r_right, to_right)
            arrived(left_land.at[step - 1, piece], s_left, r_left.at[step - 1, piece])
            left_src[step, piece] = left[part, :] + left_land[step - 1, piece]
            pass_on(step, piece, left_src, left_land, s_left, r_left, to_left)
        return 0

    lax.fori_loop(1, 7, ring_step, 0)

    right = block_stats(lax.rem(z + 1, NZ))
    for piece in range(CHUNKS):
        part = slice(piece * PIECE, (piece + 1) * PIECE)
        arrived(right_land.at[6, piece], s_right, r_right.at[6, piece])
        right_src[7, piece] = right[part, :] + right_land[6, piece]
        pass_on(7, piece, right_src, right_land, s_right, r_right, to_right)

    mass = col_scale * z_total(ITERS)
    mass_src[...] = mass
    for dy in Y_OFFSETS:
        send(mass_src, mass_land.at[dy - 1], s_mass, r_mass, at(dy=dy))
    mass_ref[y] = mass

    own = block_stats(z)
    for piece in range(CHUNKS):
        part = slice(piece * PIECE, (piece + 1) * PIECE)
        arrived(left_land.at[6, piece], s_left, r_left.at[6, piece])
        arrived(right_land.at[7, piece], s_right, r_right.at[7, piece])
        stats = own[part, :] + left_land[6, piece] + right_land[7, piece]
        scale = lax.rsqrt(jnp.mean(stats * stats, axis=1, keepdims=True) + EPSILON)
        new_ref[part, :] = stats * scale

    arrived(mass_land, s_mass, r_mass)
    for dy in Y_OFFSETS:
        mass_ref[lax.rem(y + (NY - dy), NY)] = mass_land[dy - 1]

    sent(first_land, s_first, r_first)
    sent(lab_land.at[:, k], s_lab, r_lab.at[0])
    sent(lab_land.at[:, k], s_fwd, r_fwd.at[0])
    for turn in range(ITERS + 1):
        sent(z_land.at[turn], s_z.at[turn], r_z.at[turn])
    for turn in range(ITERS):
        sent(core_land.at[turn], s_core.at[turn], r_core.at[turn])
        sent(xy_land.at[turn], s_xy.at[turn], r_xy.at[turn])
        sent(half_land.at[turn], s_half.at[turn], r_half.at[turn])
    sent(mass_land, s_mass, r_mass)
    sent(right_src, s_right, r_right.at[0, 0])
    sent(left_src, s_left, r_left.at[0, 0])


def shards(labels, counts, centroids):
    vmem = pl.BlockSpec(memory_space=pltpu.VMEM)
    dma = pltpu.SemaphoreType.DMA
    new, mass = pl.pallas_call(
        kernel,
        out_shape=(
            jax.ShapeDtypeStruct((BLOCK, FEAT), F32),
            jax.ShapeDtypeStruct((NY, 1, QUARTER), F32),
        ),
        in_specs=[pl.BlockSpec(memory_space=pltpu.SMEM), vmem, vmem],
        out_specs=(vmem, vmem),
        scratch_shapes=[
            pltpu.VMEM((KC, FEAT), BF16),
            pltpu.VMEM((KC, LAB), BF16),
            pltpu.VMEM((QUARTER, WIDE), BF16),
            pltpu.VMEM((WIDE, FEAT), BF16),
            pltpu.VMEM((2, HALF + EXTRA, FEAT), F32),
            pltpu.VMEM((NY - 1, 2, HALF + EXTRA, FEAT), F32),
            pltpu.VMEM((1, WIDE), F32),
            pltpu.VMEM((1, WIDE), F32),
            pltpu.VMEM((NY, 1, QUARTER), F32),
            pltpu.VMEM((NY - 1, 1, QUARTER), F32),
            pltpu.VMEM((ITERS + 1, 1, QUARTER), F32),
            pltpu.VMEM((ITERS + 1, NZ - 1, 1, QUARTER), F32),
            pltpu.VMEM((ITERS, 2, 1, SIDE), F32),
            pltpu.VMEM((ITERS, 1, SIDE), F32),
            pltpu.VMEM((ITERS, 1, SIDE), F32),
            pltpu.VMEM((ITERS, NY * NX - 1, 1, SIDE), F32),
            pltpu.VMEM((ITERS, 1, SIDE), F32),
            pltpu.VMEM((ITERS, 1, SIDE), F32),
            pltpu.VMEM((1, QUARTER), F32),
            pltpu.VMEM((NY - 1, 1, QUARTER), F32),
            pltpu.VMEM((8, CHUNKS, PIECE, FEAT), F32),
            pltpu.VMEM((8, CHUNKS, PIECE, FEAT), F32),
            pltpu.VMEM((7, CHUNKS, PIECE, FEAT), F32),
            pltpu.VMEM((7, CHUNKS, PIECE, FEAT), F32),
            dma, dma,
            dma, dma((NY - 1,)),
            dma, dma((NY - 1,)),
            dma((ITERS + 1,)), dma((ITERS + 1,)),
            dma((ITERS,)), dma((ITERS,)),
            dma((ITERS,)), dma((ITERS,)),
            dma((ITERS,)), dma((ITERS,)),
            dma, dma,
            dma, dma((8, CHUNKS)),
            dma, dma((7, CHUNKS)),
        ],
        compiler_params=pltpu.CompilerParams(
            collective_id=0, has_side_effects=True, vmem_limit_bytes=48 << 20
        ),
        name="sinkhorn_assign",
    )(counts, labels, centroids)
    return new, mass.reshape(KC)


def solution(mesh):
    return jax.shard_map(
        shards,
        mesh=mesh,
        in_specs=(P("label", None), P("label"), P("cent", None)),
        out_specs=(P(("cent", "label"), None), P("cent")),
        check_vma=False,
    )
```

```python
import functools
import math

import jax
import jax.numpy as jnp
from jax import lax
from jax.experimental import pallas as pl
from jax.experimental.pallas import tpu as pltpu
from jax.sharding import PartitionSpec as P

ITERS = 3
SOFTMAX_HEAT = 0.02
EPSILON = 1e-06

F32, BF16 = jnp.float32, jnp.bfloat16
MESH = pl.DeviceIdType.MESH
NT = (((1,), (1,)), ((), ()))

NY, NZ, NX, NK = 4, 16, 4, 2
LAB = 512
HALF = LAB // 2
WIDE = NY * LAB
KC = 4096
QUARTER = KC // NY
SIDE = WIDE // 2
FEAT = 256
BLOCK = QUARTER // NZ
TILE = 256
EXTRA = 8
CHUNKS = 2
STEPS = 4
PIECE = BLOCK // CHUNKS


def distance(offset, size):
    return min(offset, size - offset)


Y_OFFSETS = (2, 1, 3)
Z_OFFSETS = sorted(range(1, NZ), key=lambda d: -distance(d, NZ))
XY_OFFSETS = sorted(
    [(dy, dx) for dy in range(NY) for dx in range(NX) if dy or dx],
    key=lambda o: -(distance(o[0], NY) + distance(o[1], NX)),
)


XC_OFFSETS = sorted(
    [(dx, dk) for dx in range(NX) for dk in range(NK) if dx or dk],
    key=lambda o: -distance(o[0], NX),
)


def unit(values):
    wide = values.astype(F32)
    scale = lax.rsqrt(jnp.mean(wide * wide, axis=1, keepdims=True) + EPSILON)
    return (wide * scale).astype(BF16)


def gibbs(centroid_unit, label_unit):
    scores = lax.dot_general(centroid_unit, label_unit, NT, preferred_element_type=F32)
    return jnp.exp2(scores * (math.log2(math.e) / (SOFTMAX_HEAT * FEAT))).astype(BF16)


def split_rows(vector):
    high = vector.astype(BF16).astype(F32)
    rest = vector - high
    row = lax.broadcasted_iota(jnp.int32, (16, vector.shape[1]), 0)
    return jnp.where(row == 0, high, jnp.where(row == 1, rest, 0.0)).astype(BF16)


def joined(rows):
    return rows[0:1, :] + rows[1:2, :]


def kernel(
    counts_ref,
    lab_hbm,
    cen_hbm,
    new_ref,
    mass_ref,
    lab_ref,
    cen_ref,
    cen_unit,
    wide_gibbs,
    gibbs_t,
    lab_all,
    lab_send,
    lab_land,
    mask_all,
    row_scale,
    first_src,
    first_land,
    scale_src,
    scale_land,
    col_full,
    own_src,
    own_land,
    z_src,
    z_land,
    core_src,
    core_land,
    xy_src,
    xy_land,
    half_src,
    half_land,
    mass_src,
    mass_land,
    stat_src,
    stat_land,
    in_sem,
    s_first, r_first,
    s_lab, r_lab,
    s_fwd, r_fwd,
    s_z, r_z,
    s_core, r_core,
    s_xy, r_xy,
    s_half, r_half,
    s_mass, r_mass,
    s_scale, r_scale,
    s_own, r_own,
    s_stat, r_stat,
):
    label, cent = lax.axis_index("label"), lax.axis_index("cent")
    y, z = label // NZ, lax.rem(label, NZ)
    x, k = cent // NK, lax.rem(cent, NK)
    other = 1 - k

    copies = [pltpu.make_async_copy(lab_hbm, lab_ref, in_sem.at[NY])]
    for part in range(NY):
        rows = pl.ds(part * QUARTER, QUARTER)
        copies.append(
            pltpu.make_async_copy(cen_hbm.at[rows, :], cen_ref.at[rows, :], in_sem.at[part])
        )
    for copy in copies:
        copy.start()

    def at(dy=0, dz=0, dx=0, dk=0):
        return (
            lax.rem(y + dy, NY) * NZ + lax.rem(z + dz, NZ),
            lax.rem(x + dx, NX) * NK + lax.rem(k + dk, NK),
        )

    partner = (label, x * NK + other)

    def send(src, dst, send_sem, recv_sem, device):
        pltpu.make_async_remote_copy(
            src_ref=src,
            dst_ref=dst,
            send_sem=send_sem,
            recv_sem=recv_sem,
            device_id=device,
            device_id_type=MESH,
        ).start()

    def arrived(dst, send_sem, recv_sem):
        pltpu.make_async_remote_copy(
            src_ref=dst,
            dst_ref=dst,
            send_sem=send_sem,
            recv_sem=recv_sem,
            device_id=partner,
            device_id_type=MESH,
        ).wait_recv()

    def sent(src, send_sem, recv_sem):
        pltpu.make_async_remote_copy(
            src_ref=src,
            dst_ref=src,
            send_sem=send_sem,
            recv_sem=recv_sem,
            device_id=partner,
            device_id_type=MESH,
        ).wait_send()

    pending = []

    def sent_later(src, send_sem, recv_sem):
        pending.append(functools.partial(sent, src, send_sem, recv_sem))

    barrier = pltpu.get_barrier_semaphore()
    for dz in Z_OFFSETS:
        pl.semaphore_signal(barrier, inc=1, device_id=at(dz=dz), device_id_type=MESH)
    for dy, dx in XY_OFFSETS:
        pl.semaphore_signal(
            barrier, inc=1, device_id=at(dy=dy, dx=dx), device_id_type=MESH
        )
    for dx, dk in XC_OFFSETS:
        if dk:
            pl.semaphore_signal(
                barrier, inc=1, device_id=at(dx=dx, dk=dk), device_id_type=MESH
            )

    count = counts_ref[0]
    copies[0].wait()
    own_rows = pl.multiple_of(y * LAB, LAB)
    for half in range(2):
        rows = slice(half * HALF, (half + 1) * HALF)
        unit_half = unit(lab_ref[rows, :])
        lab_all[pl.ds(own_rows + half * HALF, HALF), :] = unit_half
        lab_send[half, 0:HALF, :] = unit_half.astype(F32)
        slot = lax.broadcasted_iota(jnp.int32, (EXTRA, HALF), 1) + half * HALF
        lab_send[half, HALF : HALF + EXTRA, :] = jnp.where(slot < count, 1.0, 0.0)
    slot = lax.broadcasted_iota(jnp.int32, (16, LAB), 1)
    own_mask = jnp.where(slot < count, 1.0, 0.0)
    mask_all[:, pl.ds(own_rows, LAB)] = own_mask[0:1, :]
    own_unit = lab_all[pl.ds(own_rows, LAB), :]

    def own_sums(turn, rows_of_scale, part, j, tile):
        sums = lax.dot_general(rows_of_scale, tile, NT, preferred_element_type=F32)
        first_src[turn, part, :, j * TILE : (j + 1) * TILE] = joined(sums)

    scale_rows = split_rows(own_mask[0:1, :])
    for part in range(NY):
        copies[part + 1].wait()
        for j in range(QUARTER // TILE):
            rows = slice(part * QUARTER + j * TILE, part * QUARTER + (j + 1) * TILE)
            tile_unit = unit(cen_ref[rows, :])
            cen_unit[rows, :] = tile_unit
            tile = gibbs(tile_unit, own_unit)
            wide_gibbs[rows, :] = tile
            own_sums(0, scale_rows, part, j, tile)

    pl.semaphore_wait(barrier, NZ - 1 + NY * NX - 1 + NX)

    def first_send(turn):
        for dy in Y_OFFSETS:
            send(
                first_src.at[turn, lax.rem(y + dy, NY)], first_land.at[turn, dy - 1],
                s_first.at[turn], r_first.at[turn], at(dy=dy),
            )
        sent_later(first_land.at[turn], s_first.at[turn], r_first.at[turn])

    def first_total(turn):
        arrived(first_land.at[turn], s_first.at[turn], r_first.at[turn])
        z_src[turn] = (
            first_src[turn, y] + first_land[turn, 0] + first_land[turn, 1] + first_land[turn, 2]
        )

    first_send(0)
    for dy in Y_OFFSETS:
        send(
            lab_send.at[k], lab_land.at[dy - 1, k],
            s_lab, r_lab.at[dy - 1], at(dy=dy),
        )
    sent_later(lab_land.at[:, k], s_lab, r_lab.at[0])

    def own_quarter(j, _):
        rows = pl.ds(pl.multiple_of(j * TILE, TILE), TILE)
        mine = pl.ds(pl.multiple_of(y * QUARTER + j * TILE, TILE), TILE)
        gibbs_t[rows, pl.ds(own_rows, LAB)] = wide_gibbs[mine, :]
        return 0

    lax.fori_loop(0, QUARTER // TILE, own_quarter, 0)

    def z_send(turn):
        for dz in Z_OFFSETS:
            send(z_src.at[turn], z_land.at[turn, dz - 1], s_z.at[turn], r_z.at[turn], at(dz=dz))
        sent_later(z_land.at[turn], s_z.at[turn], r_z.at[turn])

    def z_total(turn):
        arrived(z_land.at[turn], s_z.at[turn], r_z.at[turn])
        total = z_src[turn]
        for slot in range(NZ - 1):
            total = total + z_land[turn, slot]
        return total

    first_total(0)
    z_send(0)

    def take(dy, half):
        owner = lax.rem(y + (NY - dy), NY)
        rows = pl.ds(pl.multiple_of(owner * LAB + half * HALF, HALF), HALF)
        landed = lab_land[dy - 1, half, 0:HALF, :].astype(BF16)
        lab_all[rows, :] = landed
        mask_all[:, rows] = lab_land[dy - 1, half, HALF : HALF + 1, :]

        def tile(j, _):
            out = pl.ds(pl.multiple_of(j * TILE, TILE), TILE)
            mine = pl.ds(pl.multiple_of(y * QUARTER + j * TILE, TILE), TILE)
            gibbs_t[out, rows] = gibbs(cen_unit[mine, :], landed)
            return 0

        lax.fori_loop(0, QUARTER // TILE, tile, 0)

    def hand_over():
        for dy in (1, 3, 2):
            arrived(lab_land.at[dy - 1, k], s_lab, r_lab.at[dy - 1])
            send(
                lab_land.at[dy - 1, k], lab_land.at[dy - 1, k],
                s_fwd, r_fwd.at[dy - 1], partner,
            )
        sent_later(lab_land.at[:, k], s_fwd, r_fwd.at[0])

    def own_row_stage(col_scale):
        scale_src[...] = col_scale
        for dy in Y_OFFSETS:
            send(scale_src, scale_land.at[dy - 1], s_scale, r_scale, at(dy=dy))
        sent_later(scale_land, s_scale, r_scale)
        col_full[y] = col_scale
        arrived(scale_land, s_scale, r_scale)
        for dy in Y_OFFSETS:
            col_full[lax.rem(y + (NY - dy), NY)] = scale_land[dy - 1]
        sums = jnp.zeros((16, LAB), F32)
        for part in range(NY):
            rows = slice(part * QUARTER, (part + 1) * QUARTER)
            sums = sums + jnp.dot(
                split_rows(col_full[part]), wide_gibbs[rows, :], preferred_element_type=F32
            )
        own_src[...] = joined(sums)
        for dx, dk in XC_OFFSETS:
            send(
                own_src, own_land.at[dx * NK + dk - 1], s_own, r_own, at(dx=dx, dk=dk)
            )
        sent_later(own_land, s_own, r_own)
        hand_over()
        arrived(own_land, s_own, r_own)
        total = own_src[...]
        for slot in range(NX * NK - 1):
            total = total + own_land[slot]
        return own_mask[0:1, :] / total

    def row_stage(turn, col_scale):
        scale_rows = split_rows(col_scale)
        for half in range(2):
            columns = slice(half * SIDE, (half + 1) * SIDE)
            core_src[turn, half] = joined(
                jnp.dot(scale_rows, gibbs_t[:, columns], preferred_element_type=F32)
            )
        send(core_src.at[turn, other], core_land.at[turn], s_core.at[turn], r_core.at[turn], partner)
        sent_later(core_land.at[turn], s_core.at[turn], r_core.at[turn])
        arrived(core_land.at[turn], s_core.at[turn], r_core.at[turn])
        xy_src[turn] = core_src[turn, k] + core_land[turn]
        for dy, dx in XY_OFFSETS:
            send(
                xy_src.at[turn], xy_land.at[turn, dy * NX + dx - 1],
                s_xy.at[turn], r_xy.at[turn], at(dy=dy, dx=dx),
            )
        sent_later(xy_land.at[turn], s_xy.at[turn], r_xy.at[turn])
        arrived(xy_land.at[turn], s_xy.at[turn], r_xy.at[turn])
        total = xy_src[turn]
        for slot in range(NY * NX - 1):
            total = total + xy_land[turn, slot]
        mine = pl.ds(pl.multiple_of(k * SIDE, SIDE), SIDE)
        scale = mask_all[:, mine] / total
        half_src[turn] = scale
        send(half_src.at[turn], half_land.at[turn], s_half.at[turn], r_half.at[turn], partner)
        sent_later(half_land.at[turn], s_half.at[turn], r_half.at[turn])
        row_scale[:, mine] = scale
        arrived(half_land.at[turn], s_half.at[turn], r_half.at[turn])
        row_scale[:, pl.ds(pl.multiple_of(other * SIDE, SIDE), SIDE)] = half_land[turn]

    def col_stage(turn):
        scale_rows = split_rows(row_scale[...])
        for j in range(QUARTER // TILE):
            rows = slice(j * TILE, (j + 1) * TILE)
            z_src[turn, :, rows] = joined(
                lax.dot_general(scale_rows, gibbs_t[rows, :], NT, preferred_element_type=F32)
            )
        z_send(turn)

    col_scale = 1.0 / z_total(0)
    scale_rows = split_rows(own_row_stage(col_scale))
    for part in range(NY):
        for j in range(QUARTER // TILE):
            rows = slice(part * QUARTER + j * TILE, part * QUARTER + (j + 1) * TILE)
            own_sums(1, scale_rows, part, j, wide_gibbs[rows, :])
    first_send(1)
    for dy in (1, 3):
        take(dy, k)
    first_total(1)
    z_send(1)
    take(2, k)
    for dy in (1, 3, 2):
        arrived(lab_land.at[dy - 1, other], s_fwd, r_fwd.at[dy - 1])
        take(dy, other)
    for turn in range(1, ITERS):
        if turn > 1:
            col_stage(turn)
        col_scale = 1.0 / z_total(turn)
        row_stage(turn, col_scale)

    def block_stats(owner):
        rows = pl.ds(pl.multiple_of(owner * BLOCK, BLOCK), BLOCK)
        weights = (gibbs_t[rows, :].astype(F32) * row_scale[...]).astype(BF16)
        return jnp.dot(weights, lab_all[...], preferred_element_type=F32)

    chains = ((8, 1, 4), (7, -1, 4), (4, 1, 4), (3, -1, 3))

    def stat_step(step):
        for chain, (far, way, messages) in enumerate(chains):
            if step >= messages:
                continue
            away = way * (far - step) % NZ
            partial = block_stats(lax.rem(z + away, NZ))
            last = step == messages - 1
            device = at(dz=away if last else way % NZ)
            for piece in range(CHUNKS):
                value = partial[piece * PIECE : (piece + 1) * PIECE, :]
                if step:
                    arrived(
                        stat_land.at[chain, step - 1, piece],
                        s_stat.at[chain], r_stat.at[chain, step - 1, piece],
                    )
                    value = value + stat_land[chain, step - 1, piece]
                stat_src[chain, step, piece] = value
                send(
                    stat_src.at[chain, step, piece], stat_land.at[chain, step, piece],
                    s_stat.at[chain], r_stat.at[chain, step, piece], device,
                )

    stat_step(0)
    col_stage(ITERS)
    for step in range(1, STEPS):
        stat_step(step)
    for chain, (_, _, messages) in enumerate(chains):
        sent_later(stat_src.at[chain, 0:messages], s_stat.at[chain], r_stat.at[chain, 0, 0])

    mass = col_scale * z_total(ITERS)
    mass_src[...] = mass
    for dy in Y_OFFSETS:
        send(mass_src, mass_land.at[dy - 1], s_mass, r_mass, at(dy=dy))
    sent_later(mass_land, s_mass, r_mass)
    mass_ref[y] = mass

    own = block_stats(z)
    for piece in range(CHUNKS):
        part = slice(piece * PIECE, (piece + 1) * PIECE)
        stats = own[part, :]
        for chain in (3, 2, 1, 0):
            last = chains[chain][2] - 1
            arrived(
                stat_land.at[chain, last, piece], s_stat.at[chain], r_stat.at[chain, last, piece]
            )
            stats = stats + stat_land[chain, last, piece]
        scale = lax.rsqrt(jnp.mean(stats * stats, axis=1, keepdims=True) + EPSILON)
        new_ref[part, :] = stats * scale

    arrived(mass_land, s_mass, r_mass)
    for dy in Y_OFFSETS:
        mass_ref[lax.rem(y + (NY - dy), NY)] = mass_land[dy - 1]

    for wait in pending:
        wait()


def shards(labels, counts, centroids):
    vmem = pl.BlockSpec(memory_space=pltpu.VMEM)
    dma = pltpu.SemaphoreType.DMA
    new, mass = pl.pallas_call(
        kernel,
        out_shape=(
            jax.ShapeDtypeStruct((BLOCK, FEAT), F32),
            jax.ShapeDtypeStruct((NY, 1, QUARTER), F32),
        ),
        in_specs=[
            pl.BlockSpec(memory_space=pltpu.SMEM),
            pl.BlockSpec(memory_space=pl.ANY),
            pl.BlockSpec(memory_space=pl.ANY),
        ],
        out_specs=(vmem, vmem),
        scratch_shapes=[
            pltpu.VMEM((LAB, FEAT), BF16),
            pltpu.VMEM((KC, FEAT), BF16),
            pltpu.VMEM((KC, FEAT), BF16),
            pltpu.VMEM((KC, LAB), BF16),
            pltpu.VMEM((QUARTER, WIDE), BF16),
            pltpu.VMEM((WIDE, FEAT), BF16),
            pltpu.VMEM((2, HALF + EXTRA, FEAT), F32),
            pltpu.VMEM((NY - 1, 2, HALF + EXTRA, FEAT), F32),
            pltpu.VMEM((1, WIDE), F32),
            pltpu.VMEM((1, WIDE), F32),
            pltpu.VMEM((2, NY, 1, QUARTER), F32),
            pltpu.VMEM((2, NY - 1, 1, QUARTER), F32),
            pltpu.VMEM((1, QUARTER), F32),
            pltpu.VMEM((NY - 1, 1, QUARTER), F32),
            pltpu.VMEM((NY, 1, QUARTER), F32),
            pltpu.VMEM((1, LAB), F32),
            pltpu.VMEM((NX * NK - 1, 1, LAB), F32),
            pltpu.VMEM((ITERS + 1, 1, QUARTER), F32),
            pltpu.VMEM((ITERS + 1, NZ - 1, 1, QUARTER), F32),
            pltpu.VMEM((ITERS, 2, 1, SIDE), F32),
            pltpu.VMEM((ITERS, 1, SIDE), F32),
            pltpu.VMEM((ITERS, 1, SIDE), F32),
            pltpu.VMEM((ITERS, NY * NX - 1, 1, SIDE), F32),
            pltpu.VMEM((ITERS, 1, SIDE), F32),
            pltpu.VMEM((ITERS, 1, SIDE), F32),
            pltpu.VMEM((1, QUARTER), F32),
            pltpu.VMEM((NY - 1, 1, QUARTER), F32),
            pltpu.VMEM((4, STEPS, CHUNKS, PIECE, FEAT), F32),
            pltpu.VMEM((4, STEPS, CHUNKS, PIECE, FEAT), F32),
            dma((NY + 1,)),
            dma((2,)), dma((2,)),
            dma, dma((NY - 1,)),
            dma, dma((NY - 1,)),
            dma((ITERS + 1,)), dma((ITERS + 1,)),
            dma((ITERS,)), dma((ITERS,)),
            dma((ITERS,)), dma((ITERS,)),
            dma((ITERS,)), dma((ITERS,)),
            dma, dma,
            dma, dma,
            dma, dma,
            dma((4,)), dma((4, STEPS, CHUNKS)),
        ],
        compiler_params=pltpu.CompilerParams(
            collective_id=0, has_side_effects=True, vmem_limit_bytes=60 << 20
        ),
        name="sinkhorn_assign",
    )(counts, labels, centroids)
    return new, mass.reshape(KC)


def solution(mesh):
    return jax.shard_map(
        shards,
        mesh=mesh,
        in_specs=(P("label", None), P("label"), P("cent", None)),
        out_specs=(P(("cent", "label"), None), P("cent")),
        check_vma=False,
    )
```

```python
import functools
import math

import jax
import jax.numpy as jnp
from jax import lax
from jax.experimental import pallas as pl
from jax.experimental.pallas import tpu as pltpu
from jax.sharding import PartitionSpec as P

ITERS = 3
SOFTMAX_HEAT = 0.02
EPSILON = 1e-06

F32, BF16 = jnp.float32, jnp.bfloat16
MESH = pl.DeviceIdType.MESH
NT = (((1,), (1,)), ((), ()))

NY, NZ, NX, NK = 4, 16, 4, 2
LAB = 512
HALF = LAB // 2
WIDE = NY * LAB
KC = 4096
QUARTER = KC // NY
SIDE = WIDE // 2
FEAT = 256
BLOCK = QUARTER // NZ
TILE = 256
EXTRA = 8
CHUNKS = 2
CHAINS = ((8, 1, 4), (7, -1, 4), (4, 1, 4), (3, -1, 3))
STEPS = max(messages for _, _, messages in CHAINS)
PIECE = BLOCK // CHUNKS


def distance(offset, size):
    return min(offset, size - offset)


Y_OFFSETS = (2, 1, 3)
PART_ORDER = (2, 1, 3, 0)
Z_OFFSETS = sorted(range(1, NZ), key=lambda d: -distance(d, NZ))
XY_OFFSETS = sorted(
    [(dy, dx) for dy in range(NY) for dx in range(NX) if dy or dx],
    key=lambda o: -(distance(o[0], NY) + distance(o[1], NX)),
)


XC_OFFSETS = sorted(
    [(dx, dk) for dx in range(NX) for dk in range(NK) if dx or dk],
    key=lambda o: -distance(o[0], NX),
)


def unit(values):
    wide = values.astype(F32)
    scale = lax.rsqrt(jnp.mean(wide * wide, axis=1, keepdims=True) + EPSILON)
    return (wide * scale).astype(BF16)


def gibbs(centroid_unit, label_unit):
    scores = lax.dot_general(centroid_unit, label_unit, NT, preferred_element_type=F32)
    return jnp.exp2(scores * (math.log2(math.e) / (SOFTMAX_HEAT * FEAT))).astype(BF16)


def split_rows(vector):
    high = vector.astype(BF16).astype(F32)
    rest = vector - high
    row = lax.broadcasted_iota(jnp.int32, (16, vector.shape[1]), 0)
    return jnp.where(row == 0, high, jnp.where(row == 1, rest, 0.0)).astype(BF16)


def joined(rows):
    return rows[0:1, :] + rows[1:2, :]


def kernel(
    counts_ref,
    lab_hbm,
    cen_hbm,
    new_ref,
    mass_ref,
    lab_ref,
    cen_ref,
    cen_unit,
    wide_gibbs,
    gibbs_t,
    lab_all,
    lab_send,
    lab_land,
    mask_all,
    row_scale,
    weights,
    first_src,
    first_land,
    scale_src,
    scale_land,
    col_full,
    own_src,
    own_land,
    z_src,
    z_land,
    core_src,
    core_land,
    xy_src,
    xy_land,
    half_src,
    half_land,
    mass_src,
    mass_land,
    stat_src,
    stat_land,
    in_sem,
    s_first, r_first,
    s_lab, r_lab,
    s_fwd, r_fwd,
    s_z, r_z,
    s_core, r_core,
    s_xy, r_xy,
    s_half, r_half,
    s_mass, r_mass,
    s_scale, r_scale,
    s_own, r_own,
    s_stat, r_stat,
):
    label, cent = lax.axis_index("label"), lax.axis_index("cent")
    y, z = label // NZ, lax.rem(label, NZ)
    x, k = cent // NK, lax.rem(cent, NK)
    other = 1 - k

    copies = [pltpu.make_async_copy(lab_hbm, lab_ref, in_sem.at[NY])]
    for dy in PART_ORDER:
        rows = pl.ds(pl.multiple_of(lax.rem(y + dy, NY) * QUARTER, QUARTER), QUARTER)
        copies.append(
            pltpu.make_async_copy(cen_hbm.at[rows, :], cen_ref.at[rows, :], in_sem.at[dy])
        )
    for copy in copies:
        copy.start()

    def at(dy=0, dz=0, dx=0, dk=0):
        return (
            lax.rem(y + dy, NY) * NZ + lax.rem(z + dz, NZ),
            lax.rem(x + dx, NX) * NK + lax.rem(k + dk, NK),
        )

    partner = (label, x * NK + other)

    def send(src, dst, send_sem, recv_sem, device):
        pltpu.make_async_remote_copy(
            src_ref=src,
            dst_ref=dst,
            send_sem=send_sem,
            recv_sem=recv_sem,
            device_id=device,
            device_id_type=MESH,
        ).start()

    def arrived(dst, send_sem, recv_sem):
        pltpu.make_async_remote_copy(
            src_ref=dst,
            dst_ref=dst,
            send_sem=send_sem,
            recv_sem=recv_sem,
            device_id=partner,
            device_id_type=MESH,
        ).wait_recv()

    def sent(src, send_sem, recv_sem):
        pltpu.make_async_remote_copy(
            src_ref=src,
            dst_ref=src,
            send_sem=send_sem,
            recv_sem=recv_sem,
            device_id=partner,
            device_id_type=MESH,
        ).wait_send()

    pending = []

    def sent_later(src, send_sem, recv_sem):
        pending.append(functools.partial(sent, src, send_sem, recv_sem))

    barrier = pltpu.get_barrier_semaphore()
    for dz in Z_OFFSETS:
        pl.semaphore_signal(barrier, inc=1, device_id=at(dz=dz), device_id_type=MESH)
    for dy, dx in XY_OFFSETS:
        pl.semaphore_signal(
            barrier, inc=1, device_id=at(dy=dy, dx=dx), device_id_type=MESH
        )
    for dx, dk in XC_OFFSETS:
        if dk:
            pl.semaphore_signal(
                barrier, inc=1, device_id=at(dx=dx, dk=dk), device_id_type=MESH
            )

    count = counts_ref[0]
    copies[0].wait()
    own_rows = pl.multiple_of(y * LAB, LAB)
    for half in range(2):
        rows = slice(half * HALF, (half + 1) * HALF)
        unit_half = unit(lab_ref[rows, :])
        lab_all[pl.ds(own_rows + half * HALF, HALF), :] = unit_half
        lab_send[half, 0:HALF, :] = unit_half.astype(F32)
        slot = lax.broadcasted_iota(jnp.int32, (EXTRA, HALF), 1) + half * HALF
        lab_send[half, HALF : HALF + EXTRA, :] = jnp.where(slot < count, 1.0, 0.0)
    slot = lax.broadcasted_iota(jnp.int32, (16, LAB), 1)
    own_mask = jnp.where(slot < count, 1.0, 0.0)
    mask_all[:, pl.ds(own_rows, LAB)] = own_mask[0:1, :]
    own_unit = lab_all[pl.ds(own_rows, LAB), :]

    scale_rows = split_rows(own_mask[0:1, :])

    def first_part(dy):
        part = lax.rem(y + dy, NY)
        copies[1 + PART_ORDER.index(dy)].wait()
        for j in range(QUARTER // TILE):
            rows = pl.ds(pl.multiple_of(part * QUARTER + j * TILE, TILE), TILE)
            tile_unit = unit(cen_ref[rows, :])
            cen_unit[rows, :] = tile_unit
            tile = gibbs(tile_unit, own_unit)
            wide_gibbs[rows, :] = tile
            if dy == 0:
                gibbs_t[j * TILE : (j + 1) * TILE, pl.ds(own_rows, LAB)] = tile
            sums = lax.dot_general(scale_rows, tile, NT, preferred_element_type=F32)
            first_src[0, part, :, j * TILE : (j + 1) * TILE] = joined(sums)

    for dy in Y_OFFSETS:
        first_part(dy)
    pl.semaphore_wait(barrier, NZ - 1 + NY * NX - 1 + NX)

    def first_send(turn, dy):
        send(
            first_src.at[turn, lax.rem(y + dy, NY)], first_land.at[turn, dy - 1],
            s_first.at[turn], r_first.at[turn], at(dy=dy),
        )

    def first_total(turn):
        arrived(first_land.at[turn], s_first.at[turn], r_first.at[turn])
        z_src[turn] = (
            first_src[turn, y] + first_land[turn, 0] + first_land[turn, 1] + first_land[turn, 2]
        )

    def lab_exchange(dy):
        send(
            lab_send.at[k], lab_land.at[dy - 1, k],
            s_lab, r_lab.at[dy - 1], at(dy=dy),
        )

    for dy in Y_OFFSETS:
        first_send(0, dy)
    for dy in (1, 3):
        lab_exchange(dy)
    first_part(0)
    for turn in range(2):
        sent_later(first_land.at[turn], s_first.at[turn], r_first.at[turn])
    sent_later(lab_land.at[:, k], s_lab, r_lab.at[0])

    def z_send(turn):
        for dz in Z_OFFSETS:
            send(z_src.at[turn], z_land.at[turn, dz - 1], s_z.at[turn], r_z.at[turn], at(dz=dz))
        sent_later(z_land.at[turn], s_z.at[turn], r_z.at[turn])

    def z_total(turn):
        arrived(z_land.at[turn], s_z.at[turn], r_z.at[turn])
        total = z_src[turn]
        for slot in range(NZ - 1):
            total = total + z_land[turn, slot]
        return total

    first_total(0)
    z_send(0)

    def take(dy, half):
        owner = lax.rem(y + (NY - dy), NY)
        rows = pl.ds(pl.multiple_of(owner * LAB + half * HALF, HALF), HALF)
        landed = lab_land[dy - 1, half, 0:HALF, :].astype(BF16)
        lab_all[rows, :] = landed
        mask_all[:, rows] = lab_land[dy - 1, half, HALF : HALF + 1, :]

        def tile(j, _):
            out = pl.ds(pl.multiple_of(j * TILE, TILE), TILE)
            mine = pl.ds(pl.multiple_of(y * QUARTER + j * TILE, TILE), TILE)
            gibbs_t[out, rows] = gibbs(cen_unit[mine, :], landed)
            return 0

        lax.fori_loop(0, QUARTER // TILE, tile, 0)

    def hand_over(dy):
        arrived(lab_land.at[dy - 1, k], s_lab, r_lab.at[dy - 1])
        send(
            lab_land.at[dy - 1, k], lab_land.at[dy - 1, k],
            s_fwd, r_fwd.at[dy - 1], partner,
        )

    def other_after(dy):
        arrived(lab_land.at[dy - 1, other], s_fwd, r_fwd.at[dy - 1])
        return other

    def own_row_stage(col_scale):
        scale_src[...] = col_scale
        for dy in Y_OFFSETS:
            send(scale_src, scale_land.at[dy - 1], s_scale, r_scale, at(dy=dy))
        sent_later(scale_land, s_scale, r_scale)
        col_full[y] = col_scale
        for dy in (1, 3):
            hand_over(dy)
        arrived(scale_land, s_scale, r_scale)
        lab_exchange(2)
        for dy in Y_OFFSETS:
            col_full[lax.rem(y + (NY - dy), NY)] = scale_land[dy - 1]
        sums = jnp.zeros((16, LAB), F32)
        for part in range(NY):
            rows = slice(part * QUARTER, (part + 1) * QUARTER)
            sums = sums + jnp.dot(
                split_rows(col_full[part]), wide_gibbs[rows, :], preferred_element_type=F32
            )
        own_src[...] = joined(sums)
        for dx, dk in XC_OFFSETS:
            send(
                own_src, own_land.at[dx * NK + dk - 1], s_own, r_own, at(dx=dx, dk=dk)
            )
        sent_later(own_land, s_own, r_own)
        take(1, k)
        take(3, k)
        arrived(own_land, s_own, r_own)
        total = own_src[...]
        for slot in range(NX * NK - 1):
            total = total + own_land[slot]
        return own_mask[0:1, :] / total

    def row_stage(turn, col_scale):
        scale_rows = split_rows(col_scale)
        def half_sums(half):
            columns = pl.ds(pl.multiple_of(half * SIDE, SIDE), SIDE)
            core_src[turn, half] = joined(
                jnp.dot(scale_rows, gibbs_t[:, columns], preferred_element_type=F32)
            )

        half_sums(other)
        send(core_src.at[turn, other], core_land.at[turn], s_core.at[turn], r_core.at[turn], partner)
        half_sums(k)
        sent_later(core_land.at[turn], s_core.at[turn], r_core.at[turn])
        arrived(core_land.at[turn], s_core.at[turn], r_core.at[turn])
        xy_src[turn] = core_src[turn, k] + core_land[turn]
        for dy, dx in XY_OFFSETS:
            send(
                xy_src.at[turn], xy_land.at[turn, dy * NX + dx - 1],
                s_xy.at[turn], r_xy.at[turn], at(dy=dy, dx=dx),
            )
        sent_later(xy_land.at[turn], s_xy.at[turn], r_xy.at[turn])
        arrived(xy_land.at[turn], s_xy.at[turn], r_xy.at[turn])
        total = xy_src[turn]
        for slot in range(NY * NX - 1):
            total = total + xy_land[turn, slot]
        mine = pl.ds(pl.multiple_of(k * SIDE, SIDE), SIDE)
        scale = mask_all[:, mine] / total
        half_src[turn] = scale
        send(half_src.at[turn], half_land.at[turn], s_half.at[turn], r_half.at[turn], partner)
        sent_later(half_land.at[turn], s_half.at[turn], r_half.at[turn])
        row_scale[:, mine] = scale
        arrived(half_land.at[turn], s_half.at[turn], r_half.at[turn])
        row_scale[:, pl.ds(pl.multiple_of(other * SIDE, SIDE), SIDE)] = half_land[turn]

    def col_stage(turn):
        scale_rows = split_rows(row_scale[...])
        z_src[turn] = joined(
            lax.dot_general(scale_rows, gibbs_t[...], NT, preferred_element_type=F32)
        )
        z_send(turn)

    col_scale = 1.0 / z_total(0)
    scale_rows = split_rows(own_row_stage(col_scale))
    for dy in PART_ORDER:
        part = lax.rem(y + dy, NY)
        rows = pl.ds(pl.multiple_of(part * QUARTER, QUARTER), QUARTER)
        first_src[1, part] = joined(
            lax.dot_general(scale_rows, wide_gibbs[rows, :], NT, preferred_element_type=F32)
        )
        if dy:
            first_send(1, dy)
    take(1, other_after(1))
    first_total(1)
    z_send(1)
    take(3, other_after(3))
    hand_over(2)
    sent_later(lab_land.at[:, k], s_fwd, r_fwd.at[0])
    take(2, k)
    take(2, other_after(2))
    for turn in range(1, ITERS):
        if turn > 1:
            col_stage(turn)
        col_scale = 1.0 / z_total(turn)
        row_stage(turn, col_scale)

    def block_stats(offsets):
        for slot, offset in enumerate(offsets):
            owner = lax.rem(z + offset, NZ)
            rows = pl.ds(pl.multiple_of(owner * BLOCK, BLOCK), BLOCK)
            weights[slot * BLOCK : (slot + 1) * BLOCK, :] = (
                gibbs_t[rows, :].astype(F32) * row_scale[...]
            ).astype(BF16)
        return jnp.dot(
            weights[0 : len(offsets) * BLOCK, :], lab_all[...], preferred_element_type=F32
        )

    def stat_step(step):
        active = [c for c, (_, _, messages) in enumerate(CHAINS) if step < messages]
        away = [CHAINS[c][1] * (CHAINS[c][0] - step) % NZ for c in active]
        partial = block_stats(away + [0] * (step == STEPS - 1))
        for slot, chain in enumerate(active):
            _, way, messages = CHAINS[chain]
            device = at(dz=away[slot] if step == messages - 1 else way % NZ)
            for piece in range(CHUNKS):
                start = slot * BLOCK + piece * PIECE
                value = partial[start : start + PIECE, :]
                if step:
                    arrived(
                        stat_land.at[chain, step - 1, piece],
                        s_stat.at[chain], r_stat.at[chain, step - 1, piece],
                    )
                    value = value + stat_land[chain, step - 1, piece]
                stat_src[chain, step, piece] = value
                send(
                    stat_src.at[chain, step, piece], stat_land.at[chain, step, piece],
                    s_stat.at[chain], r_stat.at[chain, step, piece], device,
                )
        return partial[len(active) * BLOCK :, :]

    stat_step(0)
    col_stage(ITERS)
    for step in range(1, STEPS):
        own = stat_step(step)
    for chain, (_, _, messages) in enumerate(CHAINS):
        sent_later(stat_src.at[chain, 0:messages], s_stat.at[chain], r_stat.at[chain, 0, 0])

    mass = col_scale * z_total(ITERS)
    mass_src[...] = mass
    for dy in Y_OFFSETS:
        send(mass_src, mass_land.at[dy - 1], s_mass, r_mass, at(dy=dy))
    sent_later(mass_land, s_mass, r_mass)
    mass_ref[y] = mass

    for piece in range(CHUNKS):
        part = slice(piece * PIECE, (piece + 1) * PIECE)
        stats = own[part, :]
        for chain in reversed(range(len(CHAINS))):
            last = CHAINS[chain][2] - 1
            arrived(
                stat_land.at[chain, last, piece], s_stat.at[chain], r_stat.at[chain, last, piece]
            )
            stats = stats + stat_land[chain, last, piece]
        scale = lax.rsqrt(jnp.mean(stats * stats, axis=1, keepdims=True) + EPSILON)
        new_ref[part, :] = stats * scale

    arrived(mass_land, s_mass, r_mass)
    for dy in Y_OFFSETS:
        mass_ref[lax.rem(y + (NY - dy), NY)] = mass_land[dy - 1]

    for wait in pending:
        wait()


def shards(labels, counts, centroids):
    vmem = pl.BlockSpec(memory_space=pltpu.VMEM)
    dma = pltpu.SemaphoreType.DMA
    new, mass = pl.pallas_call(
        kernel,
        out_shape=(
            jax.ShapeDtypeStruct((BLOCK, FEAT), F32),
            jax.ShapeDtypeStruct((NY, 1, QUARTER), F32),
        ),
        in_specs=[
            pl.BlockSpec(memory_space=pltpu.SMEM),
            pl.BlockSpec(memory_space=pl.ANY),
            pl.BlockSpec(memory_space=pl.ANY),
        ],
        out_specs=(vmem, vmem),
        scratch_shapes=[
            pltpu.VMEM((LAB, FEAT), BF16),
            pltpu.VMEM((KC, FEAT), BF16),
            pltpu.VMEM((KC, FEAT), BF16),
            pltpu.VMEM((KC, LAB), BF16),
            pltpu.VMEM((QUARTER, WIDE), BF16),
            pltpu.VMEM((WIDE, FEAT), BF16),
            pltpu.VMEM((2, HALF + EXTRA, FEAT), F32),
            pltpu.VMEM((NY - 1, 2, HALF + EXTRA, FEAT), F32),
            pltpu.VMEM((1, WIDE), F32),
            pltpu.VMEM((1, WIDE), F32),
            pltpu.VMEM(((len(CHAINS) + 1) * BLOCK, WIDE), BF16),
            pltpu.VMEM((2, NY, 1, QUARTER), F32),
            pltpu.VMEM((2, NY - 1, 1, QUARTER), F32),
            pltpu.VMEM((1, QUARTER), F32),
            pltpu.VMEM((NY - 1, 1, QUARTER), F32),
            pltpu.VMEM((NY, 1, QUARTER), F32),
            pltpu.VMEM((1, LAB), F32),
            pltpu.VMEM((NX * NK - 1, 1, LAB), F32),
            pltpu.VMEM((ITERS + 1, 1, QUARTER), F32),
            pltpu.VMEM((ITERS + 1, NZ - 1, 1, QUARTER), F32),
            pltpu.VMEM((ITERS, 2, 1, SIDE), F32),
            pltpu.VMEM((ITERS, 1, SIDE), F32),
            pltpu.VMEM((ITERS, 1, SIDE), F32),
            pltpu.VMEM((ITERS, NY * NX - 1, 1, SIDE), F32),
            pltpu.VMEM((ITERS, 1, SIDE), F32),
            pltpu.VMEM((ITERS, 1, SIDE), F32),
            pltpu.VMEM((1, QUARTER), F32),
            pltpu.VMEM((NY - 1, 1, QUARTER), F32),
            pltpu.VMEM((len(CHAINS), STEPS, CHUNKS, PIECE, FEAT), F32),
            pltpu.VMEM((len(CHAINS), STEPS, CHUNKS, PIECE, FEAT), F32),
            dma((NY + 1,)),
            dma((2,)), dma((2,)),
            dma, dma((NY - 1,)),
            dma, dma((NY - 1,)),
            dma((ITERS + 1,)), dma((ITERS + 1,)),
            dma((ITERS,)), dma((ITERS,)),
            dma((ITERS,)), dma((ITERS,)),
            dma((ITERS,)), dma((ITERS,)),
            dma, dma,
            dma, dma,
            dma, dma,
            dma((len(CHAINS),)), dma((len(CHAINS), STEPS, CHUNKS)),
        ],
        compiler_params=pltpu.CompilerParams(
            collective_id=0, has_side_effects=True, vmem_limit_bytes=55040 << 10
        ),
        name="sinkhorn_assign",
    )(counts, labels, centroids)
    return new, mass.reshape(KC)


def solution(mesh):
    return jax.shard_map(
        shards,
        mesh=mesh,
        in_specs=(P("label", None), P("label"), P("cent", None)),
        out_specs=(P(("cent", "label"), None), P("cent")),
        check_vma=False,
    )
```

```python
import functools
import math

import jax
import jax.numpy as jnp
from jax import lax
from jax.experimental import pallas as pl
from jax.experimental.pallas import tpu as pltpu
from jax.sharding import PartitionSpec as P

ITERS = 3
SOFTMAX_HEAT = 0.02
EPSILON = 1e-06

F32, BF16 = jnp.float32, jnp.bfloat16
MESH = pl.DeviceIdType.MESH
NT = (((1,), (1,)), ((), ()))

NY, NZ, NX, NK = 4, 16, 4, 2
LAB = 512
HALF = LAB // 2
WIDE = NY * LAB
KC = 4096
QUARTER = KC // NY
SIDE = WIDE // 2
FEAT = 256
BLOCK = QUARTER // NZ
TILE = 256
EXTRA = 8
CHUNKS = 2
CHAINS = ((8, 1, 4), (7, -1, 4), (4, 1, 4), (3, -1, 3))
STEPS = max(messages for _, _, messages in CHAINS)
PIECE = BLOCK // CHUNKS


def distance(offset, size):
    return min(offset, size - offset)


Y_OFFSETS = (2, 1, 3)
PART_ORDER = (2, 1, 3, 0)
Z_OFFSETS = sorted(range(1, NZ), key=lambda d: -distance(d, NZ))
XY_OFFSETS = sorted(
    [(dy, dx) for dy in range(NY) for dx in range(NX) if dy or dx],
    key=lambda o: -(distance(o[0], NY) + distance(o[1], NX)),
)


XC_OFFSETS = sorted(
    [(dx, dk) for dx in range(NX) for dk in range(NK) if dx or dk],
    key=lambda o: -distance(o[0], NX),
)


def unit(values):
    wide = values.astype(F32)
    scale = lax.rsqrt(jnp.mean(wide * wide, axis=1, keepdims=True) + EPSILON)
    return (wide * scale).astype(BF16)


def gibbs(centroid_unit, label_unit):
    scores = lax.dot_general(centroid_unit, label_unit, NT, preferred_element_type=F32)
    return jnp.exp2(scores * (math.log2(math.e) / (SOFTMAX_HEAT * FEAT))).astype(BF16)


def split_rows(vector):
    high = vector.astype(BF16).astype(F32)
    rest = vector - high
    row = lax.broadcasted_iota(jnp.int32, (16, vector.shape[1]), 0)
    return jnp.where(row == 0, high, jnp.where(row == 1, rest, 0.0)).astype(BF16)


def joined(rows):
    return rows[0:1, :] + rows[1:2, :]


def kernel(
    counts_ref,
    lab_hbm,
    cen_hbm,
    new_ref,
    mass_ref,
    lab_ref,
    cen_ref,
    cen_unit,
    wide_gibbs,
    gibbs_t,
    lab_all,
    lab_send,
    lab_land,
    mask_all,
    row_scale,
    weights,
    first_src,
    first_land,
    scale_src,
    scale_land,
    col_full,
    own_src,
    own_land,
    z_src,
    z_land,
    core_src,
    core_land,
    xy_src,
    xy_land,
    half_src,
    half_land,
    mass_src,
    mass_land,
    stat_src,
    stat_land,
    in_sem,
    s_first, r_first,
    s_lab, r_lab,
    s_fwd, r_fwd,
    s_z, r_z,
    s_core, r_core,
    s_xy, r_xy,
    s_half, r_half,
    s_mass, r_mass,
    s_scale, r_scale,
    s_own, r_own,
    s_stat, r_stat,
):
    label, cent = lax.axis_index("label"), lax.axis_index("cent")
    y, z = label // NZ, lax.rem(label, NZ)
    x, k = cent // NK, lax.rem(cent, NK)
    other = 1 - k

    copies = [pltpu.make_async_copy(lab_hbm, lab_ref, in_sem.at[NY])]
    for dy in PART_ORDER:
        rows = pl.ds(pl.multiple_of(lax.rem(y + dy, NY) * QUARTER, QUARTER), QUARTER)
        copies.append(
            pltpu.make_async_copy(cen_hbm.at[rows, :], cen_ref.at[rows, :], in_sem.at[dy])
        )
    for copy in copies:
        copy.start()

    def at(dy=0, dz=0, dx=0, dk=0):
        return (
            lax.rem(y + dy, NY) * NZ + lax.rem(z + dz, NZ),
            lax.rem(x + dx, NX) * NK + lax.rem(k + dk, NK),
        )

    partner = (label, x * NK + other)

    def send(src, dst, send_sem, recv_sem, device):
        pltpu.make_async_remote_copy(
            src_ref=src,
            dst_ref=dst,
            send_sem=send_sem,
            recv_sem=recv_sem,
            device_id=device,
            device_id_type=MESH,
        ).start()

    def arrived(dst, send_sem, recv_sem):
        pltpu.make_async_remote_copy(
            src_ref=dst,
            dst_ref=dst,
            send_sem=send_sem,
            recv_sem=recv_sem,
            device_id=partner,
            device_id_type=MESH,
        ).wait_recv()

    def sent(src, send_sem, recv_sem):
        pltpu.make_async_remote_copy(
            src_ref=src,
            dst_ref=src,
            send_sem=send_sem,
            recv_sem=recv_sem,
            device_id=partner,
            device_id_type=MESH,
        ).wait_send()

    pending = []

    def sent_later(src, send_sem, recv_sem):
        pending.append(functools.partial(sent, src, send_sem, recv_sem))

    barrier = pltpu.get_barrier_semaphore()
    for dz in Z_OFFSETS:
        pl.semaphore_signal(barrier, inc=1, device_id=at(dz=dz), device_id_type=MESH)
    for dy, dx in XY_OFFSETS:
        pl.semaphore_signal(
            barrier, inc=1, device_id=at(dy=dy, dx=dx), device_id_type=MESH
        )
    for dx, dk in XC_OFFSETS:
        if dk:
            pl.semaphore_signal(
                barrier, inc=1, device_id=at(dx=dx, dk=dk), device_id_type=MESH
            )

    count = counts_ref[0]
    copies[0].wait()
    own_rows = pl.multiple_of(y * LAB, LAB)
    for half in range(2):
        rows = slice(half * HALF, (half + 1) * HALF)
        unit_half = unit(lab_ref[rows, :])
        lab_all[pl.ds(own_rows + half * HALF, HALF), :] = unit_half
        lab_send[half, 0:HALF, :] = unit_half.astype(F32)
        slot = lax.broadcasted_iota(jnp.int32, (EXTRA, HALF), 1) + half * HALF
        lab_send[half, HALF : HALF + EXTRA, :] = jnp.where(slot < count, 1.0, 0.0)
    slot = lax.broadcasted_iota(jnp.int32, (16, LAB), 1)
    own_mask = jnp.where(slot < count, 1.0, 0.0)
    mask_all[:, pl.ds(own_rows, LAB)] = own_mask[0:1, :]
    own_unit = lab_all[pl.ds(own_rows, LAB), :]

    scale_rows = split_rows(own_mask[0:1, :])

    def first_part(dy):
        part = lax.rem(y + dy, NY)
        copies[1 + PART_ORDER.index(dy)].wait()
        for j in range(QUARTER // TILE):
            rows = pl.ds(pl.multiple_of(part * QUARTER + j * TILE, TILE), TILE)
            tile_unit = unit(cen_ref[rows, :])
            cen_unit[rows, :] = tile_unit
            tile = gibbs(tile_unit, own_unit)
            wide_gibbs[rows, :] = tile
            if dy == 0:
                gibbs_t[j * TILE : (j + 1) * TILE, pl.ds(own_rows, LAB)] = tile
            sums = lax.dot_general(scale_rows, tile, NT, preferred_element_type=F32)
            first_src[0, part, :, j * TILE : (j + 1) * TILE] = joined(sums)

    for dy in Y_OFFSETS:
        first_part(dy)
    pl.semaphore_wait(barrier, NZ - 1 + NY * NX - 1 + NX)

    def first_send(turn, dy):
        send(
            first_src.at[turn, lax.rem(y + dy, NY)], first_land.at[turn, dy - 1],
            s_first.at[turn], r_first.at[turn], at(dy=dy),
        )

    def first_total(turn):
        arrived(first_land.at[turn], s_first.at[turn], r_first.at[turn])
        z_src[turn] = (
            first_src[turn, y] + first_land[turn, 0] + first_land[turn, 1] + first_land[turn, 2]
        )

    def lab_exchange(dy):
        send(
            lab_send.at[k], lab_land.at[dy - 1, k],
            s_lab, r_lab.at[dy - 1], at(dy=dy),
        )

    for dy in Y_OFFSETS:
        first_send(0, dy)
    for dy in (1, 3):
        lab_exchange(dy)
    first_part(0)
    for turn in range(2):
        sent_later(first_land.at[turn], s_first.at[turn], r_first.at[turn])
    sent_later(lab_land.at[:, k], s_lab, r_lab.at[0])

    def z_send(turn):
        for dz in Z_OFFSETS:
            send(z_src.at[turn], z_land.at[turn, dz - 1], s_z.at[turn], r_z.at[turn], at(dz=dz))
        sent_later(z_land.at[turn], s_z.at[turn], r_z.at[turn])

    def z_total(turn):
        arrived(z_land.at[turn], s_z.at[turn], r_z.at[turn])
        total = z_src[turn]
        for slot in range(NZ - 1):
            total = total + z_land[turn, slot]
        return total

    first_total(0)
    z_send(0)

    def take(dy, half):
        owner = lax.rem(y + (NY - dy), NY)
        rows = pl.ds(pl.multiple_of(owner * LAB + half * HALF, HALF), HALF)
        landed = lab_land[dy - 1, half, 0:HALF, :].astype(BF16)
        lab_all[rows, :] = landed
        mask_all[:, rows] = lab_land[dy - 1, half, HALF : HALF + 1, :]

        def tile(j, _):
            out = pl.ds(pl.multiple_of(j * TILE, TILE), TILE)
            mine = pl.ds(pl.multiple_of(y * QUARTER + j * TILE, TILE), TILE)
            gibbs_t[out, rows] = gibbs(cen_unit[mine, :], landed)
            return 0

        lax.fori_loop(0, QUARTER // TILE, tile, 0)

    def hand_over(dy):
        arrived(lab_land.at[dy - 1, k], s_lab, r_lab.at[dy - 1])
        send(
            lab_land.at[dy - 1, k], lab_land.at[dy - 1, k],
            s_fwd, r_fwd.at[dy - 1], partner,
        )

    def other_after(dy):
        arrived(lab_land.at[dy - 1, other], s_fwd, r_fwd.at[dy - 1])
        return other

    def own_row_stage(col_scale):
        scale_src[...] = col_scale
        for dy in Y_OFFSETS:
            send(scale_src, scale_land.at[dy - 1], s_scale, r_scale, at(dy=dy))
        sent_later(scale_land, s_scale, r_scale)
        col_full[y] = col_scale
        for dy in (1, 3):
            hand_over(dy)
        arrived(scale_land, s_scale, r_scale)
        lab_exchange(2)
        for dy in Y_OFFSETS:
            col_full[lax.rem(y + (NY - dy), NY)] = scale_land[dy - 1]
        sums = jnp.zeros((16, LAB), F32)
        for part in range(NY):
            rows = slice(part * QUARTER, (part + 1) * QUARTER)
            sums = sums + jnp.dot(
                split_rows(col_full[part]), wide_gibbs[rows, :], preferred_element_type=F32
            )
        own_src[...] = joined(sums)
        for dx, dk in XC_OFFSETS:
            send(
                own_src, own_land.at[dx * NK + dk - 1], s_own, r_own, at(dx=dx, dk=dk)
            )
        sent_later(own_land, s_own, r_own)
        take(1, k)
        take(3, k)
        arrived(own_land, s_own, r_own)
        total = own_src[...]
        for slot in range(NX * NK - 1):
            total = total + own_land[slot]
        return own_mask[0:1, :] / total

    def row_stage(turn, col_scale):
        scale_rows = split_rows(col_scale)
        def half_sums(half):
            columns = pl.ds(pl.multiple_of(half * SIDE, SIDE), SIDE)
            core_src[turn, half] = joined(
                jnp.dot(scale_rows, gibbs_t[:, columns], preferred_element_type=F32)
            )

        half_sums(other)
        send(core_src.at[turn, other], core_land.at[turn], s_core.at[turn], r_core.at[turn], partner)
        half_sums(k)
        sent_later(core_land.at[turn], s_core.at[turn], r_core.at[turn])
        arrived(core_land.at[turn], s_core.at[turn], r_core.at[turn])
        xy_src[turn] = core_src[turn, k] + core_land[turn]
        for dy, dx in XY_OFFSETS:
            send(
                xy_src.at[turn], xy_land.at[turn, dy * NX + dx - 1],
                s_xy.at[turn], r_xy.at[turn], at(dy=dy, dx=dx),
            )
        sent_later(xy_land.at[turn], s_xy.at[turn], r_xy.at[turn])
        arrived(xy_land.at[turn], s_xy.at[turn], r_xy.at[turn])
        total = xy_src[turn]
        for slot in range(NY * NX - 1):
            total = total + xy_land[turn, slot]
        mine = pl.ds(pl.multiple_of(k * SIDE, SIDE), SIDE)
        scale = mask_all[:, mine] / total
        half_src[turn] = scale
        send(half_src.at[turn], half_land.at[turn], s_half.at[turn], r_half.at[turn], partner)
        sent_later(half_land.at[turn], s_half.at[turn], r_half.at[turn])
        row_scale[:, mine] = scale
        arrived(half_land.at[turn], s_half.at[turn], r_half.at[turn])
        row_scale[:, pl.ds(pl.multiple_of(other * SIDE, SIDE), SIDE)] = half_land[turn]

    def col_stage(turn):
        scale_rows = split_rows(row_scale[...])
        z_src[turn] = joined(
            lax.dot_general(scale_rows, gibbs_t[...], NT, preferred_element_type=F32)
        )
        z_send(turn)

    col_scale = 1.0 / z_total(0)
    scale_rows = split_rows(own_row_stage(col_scale))
    for dy in PART_ORDER:
        part = lax.rem(y + dy, NY)
        rows = pl.ds(pl.multiple_of(part * QUARTER, QUARTER), QUARTER)
        first_src[1, part] = joined(
            lax.dot_general(scale_rows, wide_gibbs[rows, :], NT, preferred_element_type=F32)
        )
        if dy:
            first_send(1, dy)
    take(1, other_after(1))
    first_total(1)
    z_send(1)
    take(3, other_after(3))
    hand_over(2)
    sent_later(lab_land.at[:, k], s_fwd, r_fwd.at[0])
    take(2, k)
    take(2, other_after(2))
    for turn in range(1, ITERS):
        if turn > 1:
            col_stage(turn)
        col_scale = 1.0 / z_total(turn)
        row_stage(turn, col_scale)

    def block_stats(offsets, piece):
        for slot, offset in enumerate(offsets):
            owner = lax.rem(z + offset, NZ)
            rows = pl.ds(pl.multiple_of(owner * BLOCK + piece * PIECE, PIECE), PIECE)
            weights[piece, slot * PIECE : (slot + 1) * PIECE, :] = (
                gibbs_t[rows, :].astype(F32) * row_scale[...]
            ).astype(BF16)
        return jnp.dot(
            weights[piece, 0 : len(offsets) * PIECE, :],
            lab_all[...],
            preferred_element_type=F32,
        )

    def stat_step(step):
        active = [c for c, (_, _, messages) in enumerate(CHAINS) if step < messages]
        away = [CHAINS[c][1] * (CHAINS[c][0] - step) % NZ for c in active]
        rest = []
        for piece in range(CHUNKS):
            partial = block_stats(away + [0] * (step == STEPS - 1), piece)
            for slot, chain in enumerate(active):
                _, way, messages = CHAINS[chain]
                device = at(dz=away[slot] if step == messages - 1 else way % NZ)
                value = partial[slot * PIECE : (slot + 1) * PIECE, :]
                if step:
                    arrived(
                        stat_land.at[chain, step - 1, piece],
                        s_stat.at[chain], r_stat.at[chain, step - 1, piece],
                    )
                    value = value + stat_land[chain, step - 1, piece]
                stat_src[chain, step, piece] = value
                send(
                    stat_src.at[chain, step, piece], stat_land.at[chain, step, piece],
                    s_stat.at[chain], r_stat.at[chain, step, piece], device,
                )
            rest.append(partial[len(active) * PIECE :, :])
        return rest

    stat_step(0)
    col_stage(ITERS)
    last_sends = pending.pop()
    for wait in pending:
        wait()
    pending[:] = [last_sends]
    for step in range(1, STEPS):
        own = stat_step(step)
    for chain, (_, _, messages) in enumerate(CHAINS):
        sent_later(stat_src.at[chain, 0:messages], s_stat.at[chain], r_stat.at[chain, 0, 0])

    mass = col_scale * z_total(ITERS)
    mass_src[...] = mass
    for dy in Y_OFFSETS:
        send(mass_src, mass_land.at[dy - 1], s_mass, r_mass, at(dy=dy))
    sent_later(mass_land, s_mass, r_mass)
    mass_ref[y] = mass

    for piece in range(CHUNKS):
        part = slice(piece * PIECE, (piece + 1) * PIECE)
        stats = own[piece]
        for chain in reversed(range(len(CHAINS))):
            last = CHAINS[chain][2] - 1
            arrived(
                stat_land.at[chain, last, piece], s_stat.at[chain], r_stat.at[chain, last, piece]
            )
            stats = stats + stat_land[chain, last, piece]
        scale = lax.rsqrt(jnp.mean(stats * stats, axis=1, keepdims=True) + EPSILON)
        new_ref[part, :] = stats * scale

    arrived(mass_land, s_mass, r_mass)
    for dy in Y_OFFSETS:
        mass_ref[lax.rem(y + (NY - dy), NY)] = mass_land[dy - 1]

    for wait in pending:
        wait()


def shards(labels, counts, centroids):
    vmem = pl.BlockSpec(memory_space=pltpu.VMEM)
    dma = pltpu.SemaphoreType.DMA
    new, mass = pl.pallas_call(
        kernel,
        out_shape=(
            jax.ShapeDtypeStruct((BLOCK, FEAT), F32),
            jax.ShapeDtypeStruct((NY, 1, QUARTER), F32),
        ),
        in_specs=[
            pl.BlockSpec(memory_space=pltpu.SMEM),
            pl.BlockSpec(memory_space=pl.ANY),
            pl.BlockSpec(memory_space=pl.ANY),
        ],
        out_specs=(vmem, vmem),
        scratch_shapes=[
            pltpu.VMEM((LAB, FEAT), BF16),
            pltpu.VMEM((KC, FEAT), BF16),
            pltpu.VMEM((KC, FEAT), BF16),
            pltpu.VMEM((KC, LAB), BF16),
            pltpu.VMEM((QUARTER, WIDE), BF16),
            pltpu.VMEM((WIDE, FEAT), BF16),
            pltpu.VMEM((2, HALF + EXTRA, FEAT), F32),
            pltpu.VMEM((NY - 1, 2, HALF + EXTRA, FEAT), F32),
            pltpu.VMEM((1, WIDE), F32),
            pltpu.VMEM((1, WIDE), F32),
            pltpu.VMEM((CHUNKS, (len(CHAINS) + 1) * PIECE, WIDE), BF16),
            pltpu.VMEM((2, NY, 1, QUARTER), F32),
            pltpu.VMEM((2, NY - 1, 1, QUARTER), F32),
            pltpu.VMEM((1, QUARTER), F32),
            pltpu.VMEM((NY - 1, 1, QUARTER), F32),
            pltpu.VMEM((NY, 1, QUARTER), F32),
            pltpu.VMEM((1, LAB), F32),
            pltpu.VMEM((NX * NK - 1, 1, LAB), F32),
            pltpu.VMEM((ITERS + 1, 1, QUARTER), F32),
            pltpu.VMEM((ITERS + 1, NZ - 1, 1, QUARTER), F32),
            pltpu.VMEM((ITERS, 2, 1, SIDE), F32),
            pltpu.VMEM((ITERS, 1, SIDE), F32),
            pltpu.VMEM((ITERS, 1, SIDE), F32),
            pltpu.VMEM((ITERS, NY * NX - 1, 1, SIDE), F32),
            pltpu.VMEM((ITERS, 1, SIDE), F32),
            pltpu.VMEM((ITERS, 1, SIDE), F32),
            pltpu.VMEM((1, QUARTER), F32),
            pltpu.VMEM((NY - 1, 1, QUARTER), F32),
            pltpu.VMEM((len(CHAINS), STEPS, CHUNKS, PIECE, FEAT), F32),
            pltpu.VMEM((len(CHAINS), STEPS, CHUNKS, PIECE, FEAT), F32),
            dma((NY + 1,)),
            dma((2,)), dma((2,)),
            dma, dma((NY - 1,)),
            dma, dma((NY - 1,)),
            dma((ITERS + 1,)), dma((ITERS + 1,)),
            dma((ITERS,)), dma((ITERS,)),
            dma((ITERS,)), dma((ITERS,)),
            dma((ITERS,)), dma((ITERS,)),
            dma, dma,
            dma, dma,
            dma, dma,
            dma((len(CHAINS),)), dma((len(CHAINS), STEPS, CHUNKS)),
        ],
        compiler_params=pltpu.CompilerParams(
            collective_id=0, has_side_effects=True, vmem_limit_bytes=55040 << 10
        ),
        name="sinkhorn_assign",
    )(counts, labels, centroids)
    return new, mass.reshape(KC)


def solution(mesh):
    return jax.shard_map(
        shards,
        mesh=mesh,
        in_specs=(P("label", None), P("label"), P("cent", None)),
        out_specs=(P(("cent", "label"), None), P("cent")),
        check_vma=False,
    )
```

```python
import functools
import math

import jax
import jax.numpy as jnp
from jax import lax
from jax.experimental import pallas as pl
from jax.experimental.pallas import tpu as pltpu
from jax.sharding import PartitionSpec as P

ITERS = 3
SOFTMAX_HEAT = 0.02
EPSILON = 1e-06

F32, BF16 = jnp.float32, jnp.bfloat16
MESH = pl.DeviceIdType.MESH
NT = (((1,), (1,)), ((), ()))

NY, NZ, NX, NK = 4, 16, 4, 2
LAB = 512
HALF = LAB // 2
WIDE = NY * LAB
KC = 4096
QUARTER = KC // NY
SIDE = WIDE // 2
FEAT = 256
BLOCK = QUARTER // NZ
TILE = 256
EXTRA = 8
CHUNKS = 2
CHAINS = ((8, 1, 4), (7, -1, 4), (4, 1, 4), (3, -1, 3))
STEPS = max(messages for _, _, messages in CHAINS)
PIECE = BLOCK // CHUNKS
SHARE = HALF // NX


def distance(offset, size):
    return min(offset, size - offset)


Y_OFFSETS = (2, 1, 3)
PART_ORDER = (2, 1, 3, 0)
Z_OFFSETS = sorted(range(1, NZ), key=lambda d: -distance(d, NZ))
XY_OFFSETS = sorted(
    [(dy, dx) for dy in range(NY) for dx in range(NX) if dy or dx],
    key=lambda o: -(distance(o[0], NY) + distance(o[1], NX)),
)


X_OFFSETS = (2, 1, 3)


def unit(values):
    wide = values.astype(F32)
    scale = lax.rsqrt(jnp.mean(wide * wide, axis=1, keepdims=True) + EPSILON)
    return (wide * scale).astype(BF16)


def gibbs(centroid_unit, label_unit):
    scores = lax.dot_general(centroid_unit, label_unit, NT, preferred_element_type=F32)
    return jnp.exp2(scores * (math.log2(math.e) / (SOFTMAX_HEAT * FEAT))).astype(BF16)


def split_rows(vector):
    high = vector.astype(BF16).astype(F32)
    rest = vector - high
    row = lax.broadcasted_iota(jnp.int32, (16, vector.shape[1]), 0)
    return jnp.where(row == 0, high, jnp.where(row == 1, rest, 0.0)).astype(BF16)


def joined(rows):
    return rows[0:1, :] + rows[1:2, :]


def kernel(
    counts_ref,
    lab_hbm,
    cen_hbm,
    new_ref,
    mass_ref,
    lab_ref,
    cen_ref,
    cen_unit,
    wide_gibbs,
    gibbs_t,
    lab_all,
    lab_send,
    lab_land,
    mask_all,
    row_scale,
    weights,
    first_src,
    first_land,
    far_land,
    far_x,
    far_core,
    far_mask,
    z_src,
    z_land,
    core_src,
    core_land,
    xy_src,
    xy_land,
    half_src,
    half_land,
    mass_src,
    mass_land,
    stat_src,
    stat_land,
    in_sem,
    s_first, r_first,
    s_lab, r_lab,
    s_fwd, r_fwd,
    s_z, r_z,
    s_core, r_core,
    s_xy, r_xy,
    s_half, r_half,
    s_mass, r_mass,
    s_far, r_far,
    s_far_x, r_far_x,
    s_far_core, r_far_core,
    s_far_rest, r_far_rest,
    s_far_mask, r_far_mask,
    s_stat, r_stat,
):
    label, cent = lax.axis_index("label"), lax.axis_index("cent")
    y, z = label // NZ, lax.rem(label, NZ)
    x, k = cent // NK, lax.rem(cent, NK)
    other = 1 - k

    copies = [pltpu.make_async_copy(lab_hbm, lab_ref, in_sem.at[NY])]
    for dy in PART_ORDER:
        rows = pl.ds(pl.multiple_of(lax.rem(y + dy, NY) * QUARTER, QUARTER), QUARTER)
        copies.append(
            pltpu.make_async_copy(cen_hbm.at[rows, :], cen_ref.at[rows, :], in_sem.at[dy])
        )
    for copy in copies:
        copy.start()

    def at(dy=0, dz=0, dx=0):
        return (
            lax.rem(y + dy, NY) * NZ + lax.rem(z + dz, NZ),
            lax.rem(x + dx, NX) * NK + k,
        )

    partner = (label, x * NK + other)

    def send(src, dst, send_sem, recv_sem, device):
        pltpu.make_async_remote_copy(
            src_ref=src,
            dst_ref=dst,
            send_sem=send_sem,
            recv_sem=recv_sem,
            device_id=device,
            device_id_type=MESH,
        ).start()

    def arrived(dst, send_sem, recv_sem):
        pltpu.make_async_remote_copy(
            src_ref=dst,
            dst_ref=dst,
            send_sem=send_sem,
            recv_sem=recv_sem,
            device_id=partner,
            device_id_type=MESH,
        ).wait_recv()

    def sent(src, send_sem, recv_sem):
        pltpu.make_async_remote_copy(
            src_ref=src,
            dst_ref=src,
            send_sem=send_sem,
            recv_sem=recv_sem,
            device_id=partner,
            device_id_type=MESH,
        ).wait_send()

    pending = []

    def sent_later(src, send_sem, recv_sem):
        pending.append(functools.partial(sent, src, send_sem, recv_sem))

    barrier = pltpu.get_barrier_semaphore()
    for dz in Z_OFFSETS:
        pl.semaphore_signal(barrier, inc=1, device_id=at(dz=dz), device_id_type=MESH)
    for dy, dx in XY_OFFSETS:
        pl.semaphore_signal(
            barrier, inc=1, device_id=at(dy=dy, dx=dx), device_id_type=MESH
        )
    pl.semaphore_signal(barrier, inc=1, device_id=partner, device_id_type=MESH)

    count = counts_ref[0]
    copies[0].wait()
    own_rows = pl.multiple_of(y * LAB, LAB)
    for half in range(2):
        rows = slice(half * HALF, (half + 1) * HALF)
        unit_half = unit(lab_ref[rows, :])
        lab_all[pl.ds(own_rows + half * HALF, HALF), :] = unit_half
        lab_send[half, 0:HALF, :] = unit_half.astype(F32)
        slot = lax.broadcasted_iota(jnp.int32, (EXTRA, HALF), 1) + half * HALF
        lab_send[half, HALF : HALF + EXTRA, :] = jnp.where(slot < count, 1.0, 0.0)
    slot = lax.broadcasted_iota(jnp.int32, (16, LAB), 1)
    own_mask = jnp.where(slot < count, 1.0, 0.0)
    mask_all[:, pl.ds(own_rows, LAB)] = own_mask[0:1, :]
    own_unit = lab_all[pl.ds(own_rows, LAB), :]

    scale_rows = split_rows(own_mask[0:1, :])

    def first_part(dy):
        part = lax.rem(y + dy, NY)
        copies[1 + PART_ORDER.index(dy)].wait()
        for j in range(QUARTER // TILE):
            rows = pl.ds(pl.multiple_of(part * QUARTER + j * TILE, TILE), TILE)
            tile_unit = unit(cen_ref[rows, :])
            cen_unit[rows, :] = tile_unit
            tile = gibbs(tile_unit, own_unit)
            wide_gibbs[rows, :] = tile
            if dy == 0:
                gibbs_t[j * TILE : (j + 1) * TILE, pl.ds(own_rows, LAB)] = tile
            sums = lax.dot_general(scale_rows, tile, NT, preferred_element_type=F32)
            first_src[part, :, j * TILE : (j + 1) * TILE] = joined(sums)

    for dy in Y_OFFSETS:
        first_part(dy)
    pl.semaphore_wait(barrier, NZ - 1 + NY * NX - 1 + 1)

    def lab_exchange(dy):
        send(
            lab_send.at[k], lab_land.at[dy // 2, k],
            s_lab, r_lab.at[dy // 2], at(dy=dy),
        )

    for dy in Y_OFFSETS:
        send(
            first_src.at[lax.rem(y + dy, NY)], first_land.at[dy - 1],
            s_first, r_first, at(dy=dy),
        )
    send(
        lab_send.at[k, pl.ds(pl.multiple_of(x * SHARE, SHARE), SHARE), :], far_land,
        s_far, r_far, at(dy=2),
    )
    send(lab_send.at[:, HALF : HALF + EXTRA, :], far_mask, s_far_mask, r_far_mask, at(dy=2))
    for dy in (1, 3):
        lab_exchange(dy)
    first_part(0)
    sent_later(first_land, s_first, r_first)
    sent_later(far_land, s_far, r_far)
    sent_later(far_mask, s_far_mask, r_far_mask)
    sent_later(lab_land.at[:, k], s_lab, r_lab.at[0])

    def z_send(turn):
        for dz in Z_OFFSETS:
            send(z_src.at[turn], z_land.at[turn, dz - 1], s_z.at[turn], r_z.at[turn], at(dz=dz))
        sent_later(z_land.at[turn], s_z.at[turn], r_z.at[turn])

    def z_total(turn):
        arrived(z_land.at[turn], s_z.at[turn], r_z.at[turn])
        total = z_src[turn]
        for slot in range(NZ - 1):
            total = total + z_land[turn, slot]
        return total

    arrived(first_land, s_first, r_first)
    z_src[0] = first_src[y] + first_land[0] + first_land[1] + first_land[2]
    z_send(0)

    arrived(far_land, s_far, r_far)
    for dx in X_OFFSETS:
        send(far_land, far_x.at[dx - 1], s_far_x, r_far_x, at(dx=dx))
    send(far_land, far_core.at[0], s_far_core, r_far_core, partner)
    sent_later(far_x, s_far_x, r_far_x)
    sent_later(far_land, s_far_core, r_far_core)

    def fill(owner, half):
        rows = pl.ds(pl.multiple_of(owner * LAB + half * HALF, HALF), HALF)
        for j in range(QUARTER // TILE):
            mine = pl.ds(pl.multiple_of(y * QUARTER + j * TILE, TILE), TILE)
            gibbs_t[j * TILE : (j + 1) * TILE, rows] = gibbs(cen_unit[mine, :], lab_all[rows, :])

    def take(dy, half):
        owner = lax.rem(y + (NY - dy), NY)
        rows = pl.ds(pl.multiple_of(owner * LAB + half * HALF, HALF), HALF)
        lab_all[rows, :] = lab_land[dy // 2, half, 0:HALF, :].astype(BF16)
        mask_all[:, rows] = lab_land[dy // 2, half, HALF : HALF + 1, :]
        fill(owner, half)

    def take_far(half, quarters):
        owner = lax.rem(y + 2, NY)
        start = owner * LAB + half * HALF
        for dx, quarter in enumerate(quarters):
            first = start + lax.rem(x + (NX - dx), NX) * SHARE
            lab_all[pl.ds(pl.multiple_of(first, SHARE), SHARE), :] = quarter[...].astype(BF16)
        mask_all[:, pl.ds(pl.multiple_of(start, HALF), HALF)] = far_mask[half, 0:1, :]
        fill(owner, half)

    def hand_over(dy):
        arrived(lab_land.at[dy // 2, k], s_lab, r_lab.at[dy // 2])
        send(
            lab_land.at[dy // 2, k], lab_land.at[dy // 2, k],
            s_fwd, r_fwd.at[dy // 2], partner,
        )

    def other_after(dy):
        arrived(lab_land.at[dy // 2, other], s_fwd, r_fwd.at[dy // 2])
        return other

    for dy in (1, 3):
        hand_over(dy)
    arrived(far_x, s_far_x, r_far_x)
    send(far_x, far_core.at[1:NX], s_far_rest, r_far_rest, partner)
    sent_later(lab_land.at[:, k], s_fwd, r_fwd.at[0])
    sent_later(far_x, s_far_rest, r_far_rest)
    take(1, k)
    take(3, k)
    arrived(far_mask, s_far_mask, r_far_mask)
    take_far(k, [far_land] + [far_x.at[dx - 1] for dx in range(1, NX)])
    for dy in (1, 3):
        take(dy, other_after(dy))
    arrived(far_core.at[0], s_far_core, r_far_core)
    arrived(far_core.at[1:NX], s_far_rest, r_far_rest)
    take_far(other, [far_core.at[dx] for dx in range(NX)])

    def row_stage(turn, col_scale):
        scale_rows = split_rows(col_scale)
        def half_sums(half):
            columns = pl.ds(pl.multiple_of(half * SIDE, SIDE), SIDE)
            core_src[turn, half] = joined(
                jnp.dot(scale_rows, gibbs_t[:, columns], preferred_element_type=F32)
            )

        half_sums(other)
        send(core_src.at[turn, other], core_land.at[turn], s_core.at[turn], r_core.at[turn], partner)
        half_sums(k)
        sent_later(core_land.at[turn], s_core.at[turn], r_core.at[turn])
        arrived(core_land.at[turn], s_core.at[turn], r_core.at[turn])
        xy_src[turn] = core_src[turn, k] + core_land[turn]
        for dy, dx in XY_OFFSETS:
            send(
                xy_src.at[turn], xy_land.at[turn, dy * NX + dx - 1],
                s_xy.at[turn], r_xy.at[turn], at(dy=dy, dx=dx),
            )
        sent_later(xy_land.at[turn], s_xy.at[turn], r_xy.at[turn])
        arrived(xy_land.at[turn], s_xy.at[turn], r_xy.at[turn])
        total = xy_src[turn]
        for slot in range(NY * NX - 1):
            total = total + xy_land[turn, slot]
        mine = pl.ds(pl.multiple_of(k * SIDE, SIDE), SIDE)
        scale = mask_all[:, mine] / total
        half_src[turn] = scale
        send(half_src.at[turn], half_land.at[turn], s_half.at[turn], r_half.at[turn], partner)
        sent_later(half_land.at[turn], s_half.at[turn], r_half.at[turn])
        row_scale[:, mine] = scale
        arrived(half_land.at[turn], s_half.at[turn], r_half.at[turn])
        row_scale[:, pl.ds(pl.multiple_of(other * SIDE, SIDE), SIDE)] = half_land[turn]

    def col_stage(turn):
        scale_rows = split_rows(row_scale[...])
        z_src[turn] = joined(
            lax.dot_general(scale_rows, gibbs_t[...], NT, preferred_element_type=F32)
        )
        z_send(turn)

    col_scale = 1.0 / z_total(0)
    for turn in range(ITERS):
        if turn:
            col_stage(turn)
            col_scale = 1.0 / z_total(turn)
        row_stage(turn, col_scale)

    def block_stats(offsets, piece):
        for slot, offset in enumerate(offsets):
            owner = lax.rem(z + offset, NZ)
            rows = pl.ds(pl.multiple_of(owner * BLOCK + piece * PIECE, PIECE), PIECE)
            weights[piece, slot * PIECE : (slot + 1) * PIECE, :] = (
                gibbs_t[rows, :].astype(F32) * row_scale[...]
            ).astype(BF16)
        return jnp.dot(
            weights[piece, 0 : len(offsets) * PIECE, :],
            lab_all[...],
            preferred_element_type=F32,
        )

    def stat_step(step):
        active = [c for c, (_, _, messages) in enumerate(CHAINS) if step < messages]
        away = [CHAINS[c][1] * (CHAINS[c][0] - step) % NZ for c in active]
        rest = []
        for piece in range(CHUNKS):
            partial = block_stats(away + [0] * (step == STEPS - 1), piece)
            for slot, chain in enumerate(active):
                _, way, messages = CHAINS[chain]
                device = at(dz=away[slot] if step == messages - 1 else way % NZ)
                value = partial[slot * PIECE : (slot + 1) * PIECE, :]
                if step:
                    arrived(
                        stat_land.at[chain, step - 1, piece],
                        s_stat.at[chain], r_stat.at[chain, step - 1, piece],
                    )
                    value = value + stat_land[chain, step - 1, piece]
                stat_src[chain, step, piece] = value
                send(
                    stat_src.at[chain, step, piece], stat_land.at[chain, step, piece],
                    s_stat.at[chain], r_stat.at[chain, step, piece], device,
                )
            rest.append(partial[len(active) * PIECE :, :])
        return rest

    stat_step(0)
    col_stage(ITERS)
    last_sends = pending.pop()
    for wait in pending:
        wait()
    pending[:] = [last_sends]
    for step in range(1, STEPS):
        own = stat_step(step)
    for chain, (_, _, messages) in enumerate(CHAINS):
        sent_later(stat_src.at[chain, 0:messages], s_stat.at[chain], r_stat.at[chain, 0, 0])

    mass = col_scale * z_total(ITERS)
    mass_src[...] = mass
    for dy in Y_OFFSETS:
        send(mass_src, mass_land.at[dy - 1], s_mass, r_mass, at(dy=dy))
    sent_later(mass_land, s_mass, r_mass)
    mass_ref[y] = mass

    for piece in range(CHUNKS):
        part = slice(piece * PIECE, (piece + 1) * PIECE)
        stats = own[piece]
        for chain in reversed(range(len(CHAINS))):
            last = CHAINS[chain][2] - 1
            arrived(
                stat_land.at[chain, last, piece], s_stat.at[chain], r_stat.at[chain, last, piece]
            )
            stats = stats + stat_land[chain, last, piece]
        scale = lax.rsqrt(jnp.mean(stats * stats, axis=1, keepdims=True) + EPSILON)
        new_ref[part, :] = stats * scale

    arrived(mass_land, s_mass, r_mass)
    for dy in Y_OFFSETS:
        mass_ref[lax.rem(y + (NY - dy), NY)] = mass_land[dy - 1]

    for wait in pending:
        wait()


def shards(labels, counts, centroids):
    vmem = pl.BlockSpec(memory_space=pltpu.VMEM)
    dma = pltpu.SemaphoreType.DMA
    new, mass = pl.pallas_call(
        kernel,
        out_shape=(
            jax.ShapeDtypeStruct((BLOCK, FEAT), F32),
            jax.ShapeDtypeStruct((NY, 1, QUARTER), F32),
        ),
        in_specs=[
            pl.BlockSpec(memory_space=pltpu.SMEM),
            pl.BlockSpec(memory_space=pl.ANY),
            pl.BlockSpec(memory_space=pl.ANY),
        ],
        out_specs=(vmem, vmem),
        scratch_shapes=[
            pltpu.VMEM((LAB, FEAT), BF16),
            pltpu.VMEM((KC, FEAT), BF16),
            pltpu.VMEM((KC, FEAT), BF16),
            pltpu.VMEM((KC, LAB), BF16),
            pltpu.VMEM((QUARTER, WIDE), BF16),
            pltpu.VMEM((WIDE, FEAT), BF16),
            pltpu.VMEM((2, HALF + EXTRA, FEAT), F32),
            pltpu.VMEM((2, 2, HALF + EXTRA, FEAT), F32),
            pltpu.VMEM((1, WIDE), F32),
            pltpu.VMEM((1, WIDE), F32),
            pltpu.VMEM((CHUNKS, (len(CHAINS) + 1) * PIECE, WIDE), BF16),
            pltpu.VMEM((NY, 1, QUARTER), F32),
            pltpu.VMEM((NY - 1, 1, QUARTER), F32),
            pltpu.VMEM((SHARE, FEAT), F32),
            pltpu.VMEM((NX - 1, SHARE, FEAT), F32),
            pltpu.VMEM((NX, SHARE, FEAT), F32),
            pltpu.VMEM((2, EXTRA, FEAT), F32),
            pltpu.VMEM((ITERS + 1, 1, QUARTER), F32),
            pltpu.VMEM((ITERS + 1, NZ - 1, 1, QUARTER), F32),
            pltpu.VMEM((ITERS, 2, 1, SIDE), F32),
            pltpu.VMEM((ITERS, 1, SIDE), F32),
            pltpu.VMEM((ITERS, 1, SIDE), F32),
            pltpu.VMEM((ITERS, NY * NX - 1, 1, SIDE), F32),
            pltpu.VMEM((ITERS, 1, SIDE), F32),
            pltpu.VMEM((ITERS, 1, SIDE), F32),
            pltpu.VMEM((1, QUARTER), F32),
            pltpu.VMEM((NY - 1, 1, QUARTER), F32),
            pltpu.VMEM((len(CHAINS), STEPS, CHUNKS, PIECE, FEAT), F32),
            pltpu.VMEM((len(CHAINS), STEPS, CHUNKS, PIECE, FEAT), F32),
            dma((NY + 1,)),
            dma, dma,
            dma, dma((2,)),
            dma, dma((2,)),
            dma((ITERS + 1,)), dma((ITERS + 1,)),
            dma((ITERS,)), dma((ITERS,)),
            dma((ITERS,)), dma((ITERS,)),
            dma((ITERS,)), dma((ITERS,)),
            dma, dma,
            dma, dma,
            dma, dma,
            dma, dma,
            dma, dma,
            dma, dma,
            dma((len(CHAINS),)), dma((len(CHAINS), STEPS, CHUNKS)),
        ],
        compiler_params=pltpu.CompilerParams(
            collective_id=0, has_side_effects=True, vmem_limit_bytes=55040 << 10
        ),
        name="sinkhorn_assign",
    )(counts, labels, centroids)
    return new, mass.reshape(KC)


def solution(mesh):
    return jax.shard_map(
        shards,
        mesh=mesh,
        in_specs=(P("label", None), P("label"), P("cent", None)),
        out_specs=(P(("cent", "label"), None), P("cent")),
        check_vma=False,
    )
```

```python
import functools
import math

import jax
import jax.numpy as jnp
from jax import lax
from jax.experimental import pallas as pl
from jax.experimental.pallas import tpu as pltpu
from jax.sharding import PartitionSpec as P

ITERS = 3
SOFTMAX_HEAT = 0.02
EPSILON = 1e-06

F32, BF16 = jnp.float32, jnp.bfloat16
MESH = pl.DeviceIdType.MESH
NT = (((1,), (1,)), ((), ()))

NY, NZ, NX, NK = 4, 16, 4, 2
LAB = 512
HALF = LAB // 2
WIDE = NY * LAB
KC = 4096
QUARTER = KC // NY
SIDE = WIDE // 2
FEAT = 256
BLOCK = QUARTER // NZ
TILE = 256
EXTRA = 8
CHUNKS = 2
CHAINS = ((8, 1, 4), (7, -1, 4), (4, 1, 4), (3, -1, 3))
STEPS = max(messages for _, _, messages in CHAINS)
PIECE = BLOCK // CHUNKS
QUAD = 4
SHARE = HALF // NX


def distance(offset, size):
    return min(offset, size - offset)


Y_OFFSETS = (2, 1, 3)
PART_ORDER = (2, 1, 3, 0)
Z_OFFSETS = sorted(range(1, NZ), key=lambda d: -distance(d, NZ))
XY_OFFSETS = sorted(
    [(dy, dx) for dy in range(NY) for dx in range(NX) if dy or dx],
    key=lambda o: -(distance(o[0], NY) + distance(o[1], NX)),
)


X_OFFSETS = (2, 1, 3)


def unit(values):
    wide = values.astype(F32)
    scale = lax.rsqrt(jnp.mean(wide * wide, axis=1, keepdims=True) + EPSILON)
    return (wide * scale).astype(BF16)


def gibbs(centroid_unit, label_unit):
    scores = lax.dot_general(centroid_unit, label_unit, NT, preferred_element_type=F32)
    return jnp.exp2(scores * (math.log2(math.e) / (SOFTMAX_HEAT * FEAT))).astype(BF16)


def split_rows(vector):
    high = vector.astype(BF16).astype(F32)
    rest = vector - high
    row = lax.broadcasted_iota(jnp.int32, (16, vector.shape[1]), 0)
    return jnp.where(row == 0, high, jnp.where(row == 1, rest, 0.0)).astype(BF16)


def joined(rows):
    return rows[0:1, :] + rows[1:2, :]


def kernel(
    counts_ref,
    lab_hbm,
    cen_hbm,
    new_ref,
    mass_ref,
    lab_ref,
    cen_ref,
    cen_unit,
    wide_gibbs,
    gibbs_t,
    lab_all,
    lab_send,
    lab_land,
    mask_all,
    row_scale,
    weights,
    first_src,
    first_land,
    far_land,
    far_x,
    far_core,
    far_mask,
    z_src,
    z_land,
    core_src,
    core_land,
    xy_src,
    xy_land,
    half_src,
    half_land,
    quad_land,
    ring_src,
    ring_land,
    mass_src,
    mass_land,
    stat_src,
    stat_land,
    in_sem,
    s_first, r_first,
    s_lab, r_lab,
    s_fwd, r_fwd,
    s_z, r_z,
    s_core, r_core,
    s_xy, r_xy,
    s_half, r_half,
    s_quad, r_quad,
    s_ring, r_ring,
    s_mass, r_mass,
    s_far, r_far,
    s_far_x, r_far_x,
    s_far_core, r_far_core,
    s_far_rest, r_far_rest,
    s_far_mask, r_far_mask,
    s_stat, r_stat,
):
    label, cent = lax.axis_index("label"), lax.axis_index("cent")
    y, z = label // NZ, lax.rem(label, NZ)
    x, k = cent // NK, lax.rem(cent, NK)
    other = 1 - k

    copies = [pltpu.make_async_copy(lab_hbm, lab_ref, in_sem.at[NY])]
    for dy in PART_ORDER:
        rows = pl.ds(pl.multiple_of(lax.rem(y + dy, NY) * QUARTER, QUARTER), QUARTER)
        copies.append(
            pltpu.make_async_copy(cen_hbm.at[rows, :], cen_ref.at[rows, :], in_sem.at[dy])
        )
    for copy in copies:
        copy.start()

    def at(dy=0, dz=0, dx=0):
        return (
            lax.rem(y + dy, NY) * NZ + lax.rem(z + dz, NZ),
            lax.rem(x + dx, NX) * NK + k,
        )

    partner = (label, x * NK + other)

    def send(src, dst, send_sem, recv_sem, device):
        pltpu.make_async_remote_copy(
            src_ref=src,
            dst_ref=dst,
            send_sem=send_sem,
            recv_sem=recv_sem,
            device_id=device,
            device_id_type=MESH,
        ).start()

    def arrived(dst, send_sem, recv_sem):
        pltpu.make_async_remote_copy(
            src_ref=dst,
            dst_ref=dst,
            send_sem=send_sem,
            recv_sem=recv_sem,
            device_id=partner,
            device_id_type=MESH,
        ).wait_recv()

    def sent(src, send_sem, recv_sem):
        pltpu.make_async_remote_copy(
            src_ref=src,
            dst_ref=src,
            send_sem=send_sem,
            recv_sem=recv_sem,
            device_id=partner,
            device_id_type=MESH,
        ).wait_send()

    pending = []

    def sent_later(src, send_sem, recv_sem):
        pending.append(functools.partial(sent, src, send_sem, recv_sem))

    barrier = pltpu.get_barrier_semaphore()
    for dz in Z_OFFSETS:
        pl.semaphore_signal(barrier, inc=1, device_id=at(dz=dz), device_id_type=MESH)
    for dy, dx in XY_OFFSETS:
        pl.semaphore_signal(
            barrier, inc=1, device_id=at(dy=dy, dx=dx), device_id_type=MESH
        )
    pl.semaphore_signal(barrier, inc=1, device_id=partner, device_id_type=MESH)

    count = counts_ref[0]
    copies[0].wait()
    own_rows = pl.multiple_of(y * LAB, LAB)
    for half in range(2):
        rows = slice(half * HALF, (half + 1) * HALF)
        unit_half = unit(lab_ref[rows, :])
        lab_all[pl.ds(own_rows + half * HALF, HALF), :] = unit_half
        lab_send[half, 0:HALF, :] = unit_half.astype(F32)
        slot = lax.broadcasted_iota(jnp.int32, (EXTRA, HALF), 1) + half * HALF
        lab_send[half, HALF : HALF + EXTRA, :] = jnp.where(slot < count, 1.0, 0.0)
    slot = lax.broadcasted_iota(jnp.int32, (16, LAB), 1)
    own_mask = jnp.where(slot < count, 1.0, 0.0)
    mask_all[:, pl.ds(own_rows, LAB)] = own_mask[0:1, :]
    own_unit = lab_all[pl.ds(own_rows, LAB), :]

    scale_rows = split_rows(own_mask[0:1, :])

    def first_part(dy):
        part = lax.rem(y + dy, NY)
        copies[1 + PART_ORDER.index(dy)].wait()
        for j in range(QUARTER // TILE):
            rows = pl.ds(pl.multiple_of(part * QUARTER + j * TILE, TILE), TILE)
            tile_unit = unit(cen_ref[rows, :])
            cen_unit[rows, :] = tile_unit
            tile = gibbs(tile_unit, own_unit)
            wide_gibbs[rows, :] = tile
            if dy == 0:
                gibbs_t[j * TILE : (j + 1) * TILE, pl.ds(own_rows, LAB)] = tile
            sums = lax.dot_general(scale_rows, tile, NT, preferred_element_type=F32)
            first_src[part, :, j * TILE : (j + 1) * TILE] = joined(sums)

    for dy in Y_OFFSETS:
        first_part(dy)
    pl.semaphore_wait(barrier, NZ - 1 + NY * NX - 1 + 1)

    def lab_exchange(dy):
        send(
            lab_send.at[k], lab_land.at[dy // 2, k],
            s_lab, r_lab.at[dy // 2], at(dy=dy),
        )

    for dy in Y_OFFSETS:
        send(
            first_src.at[lax.rem(y + dy, NY)], first_land.at[dy - 1],
            s_first, r_first, at(dy=dy),
        )
    send(
        lab_send.at[k, pl.ds(pl.multiple_of(x * SHARE, SHARE), SHARE), :], far_land,
        s_far, r_far, at(dy=2),
    )
    send(lab_send.at[:, HALF : HALF + EXTRA, :], far_mask, s_far_mask, r_far_mask, at(dy=2))
    for dy in (1, 3):
        lab_exchange(dy)
    first_part(0)
    sent_later(first_land, s_first, r_first)
    sent_later(far_land, s_far, r_far)
    sent_later(far_mask, s_far_mask, r_far_mask)
    sent_later(lab_land.at[:, k], s_lab, r_lab.at[0])

    def z_send(turn):
        for dz in Z_OFFSETS:
            send(z_src.at[turn], z_land.at[turn, dz - 1], s_z.at[turn], r_z.at[turn], at(dz=dz))
        sent_later(z_land.at[turn], s_z.at[turn], r_z.at[turn])

    def z_total(turn):
        arrived(z_land.at[turn], s_z.at[turn], r_z.at[turn])
        total = z_src[turn]
        for slot in range(NZ - 1):
            total = total + z_land[turn, slot]
        return total

    arrived(first_land, s_first, r_first)
    z_src[0] = first_src[y] + first_land[0] + first_land[1] + first_land[2]
    z_send(0)

    arrived(far_land, s_far, r_far)
    for dx in X_OFFSETS:
        send(far_land, far_x.at[dx - 1], s_far_x, r_far_x, at(dx=dx))
    send(far_land, far_core.at[0], s_far_core, r_far_core, partner)
    sent_later(far_x, s_far_x, r_far_x)
    sent_later(far_land, s_far_core, r_far_core)

    def fill(owner, half):
        rows = pl.ds(pl.multiple_of(owner * LAB + half * HALF, HALF), HALF)
        for j in range(QUARTER // TILE):
            mine = pl.ds(pl.multiple_of(y * QUARTER + j * TILE, TILE), TILE)
            gibbs_t[j * TILE : (j + 1) * TILE, rows] = gibbs(cen_unit[mine, :], lab_all[rows, :])

    def take(dy, half):
        owner = lax.rem(y + (NY - dy), NY)
        rows = pl.ds(pl.multiple_of(owner * LAB + half * HALF, HALF), HALF)
        lab_all[rows, :] = lab_land[dy // 2, half, 0:HALF, :].astype(BF16)
        mask_all[:, rows] = lab_land[dy // 2, half, HALF : HALF + 1, :]
        fill(owner, half)

    def take_far(half, quarters):
        owner = lax.rem(y + 2, NY)
        start = owner * LAB + half * HALF
        for dx, quarter in enumerate(quarters):
            first = start + lax.rem(x + (NX - dx), NX) * SHARE
            lab_all[pl.ds(pl.multiple_of(first, SHARE), SHARE), :] = quarter[...].astype(BF16)
        mask_all[:, pl.ds(pl.multiple_of(start, HALF), HALF)] = far_mask[half, 0:1, :]
        fill(owner, half)

    def hand_over(dy):
        arrived(lab_land.at[dy // 2, k], s_lab, r_lab.at[dy // 2])
        send(
            lab_land.at[dy // 2, k], lab_land.at[dy // 2, k],
            s_fwd, r_fwd.at[dy // 2], partner,
        )

    def other_after(dy):
        arrived(lab_land.at[dy // 2, other], s_fwd, r_fwd.at[dy // 2])
        return other

    for dy in (1, 3):
        hand_over(dy)
    arrived(far_x, s_far_x, r_far_x)
    send(far_x, far_core.at[1:NX], s_far_rest, r_far_rest, partner)
    sent_later(lab_land.at[:, k], s_fwd, r_fwd.at[0])
    sent_later(far_x, s_far_rest, r_far_rest)
    take(1, k)
    take(3, k)
    arrived(far_mask, s_far_mask, r_far_mask)
    take_far(k, [far_land] + [far_x.at[dx - 1] for dx in range(1, NX)])
    for dy in (1, 3):
        take(dy, other_after(dy))
    arrived(far_core.at[0], s_far_core, r_far_core)
    arrived(far_core.at[1:NX], s_far_rest, r_far_rest)
    take_far(other, [far_core.at[dx] for dx in range(NX)])

    def row_stage(turn, col_scale):
        scale_rows = split_rows(col_scale)
        def half_sums(half):
            columns = pl.ds(pl.multiple_of(half * SIDE, SIDE), SIDE)
            core_src[turn, half] = joined(
                jnp.dot(scale_rows, gibbs_t[:, columns], preferred_element_type=F32)
            )

        half_sums(other)
        send(core_src.at[turn, other], core_land.at[turn], s_core.at[turn], r_core.at[turn], partner)
        half_sums(k)
        sent_later(core_land.at[turn], s_core.at[turn], r_core.at[turn])
        arrived(core_land.at[turn], s_core.at[turn], r_core.at[turn])
        xy_src[turn] = core_src[turn, k] + core_land[turn]
        for dy, dx in XY_OFFSETS:
            send(
                xy_src.at[turn], xy_land.at[turn, dy * NX + dx - 1],
                s_xy.at[turn], r_xy.at[turn], at(dy=dy, dx=dx),
            )
        sent_later(xy_land.at[turn], s_xy.at[turn], r_xy.at[turn])
        arrived(xy_land.at[turn], s_xy.at[turn], r_xy.at[turn])
        total = xy_src[turn]
        for slot in range(NY * NX - 1):
            total = total + xy_land[turn, slot]
        mine = pl.ds(pl.multiple_of(k * SIDE, SIDE), SIDE)
        scale = mask_all[:, mine] / total
        half_src[turn] = scale
        send(half_src.at[turn], half_land.at[turn], s_half.at[turn], r_half.at[turn], partner)
        sent_later(half_land.at[turn], s_half.at[turn], r_half.at[turn])
        row_scale[:, mine] = scale
        arrived(half_land.at[turn], s_half.at[turn], r_half.at[turn])
        row_scale[:, pl.ds(pl.multiple_of(other * SIDE, SIDE), SIDE)] = half_land[turn]

    def col_stage(turn):
        scale_rows = split_rows(row_scale[...])
        z_src[turn] = joined(
            lax.dot_general(scale_rows, gibbs_t[...], NT, preferred_element_type=F32)
        )

    col_scale = 1.0 / z_total(0)
    for turn in range(ITERS):
        if turn:
            col_stage(turn)
            z_send(turn)
            col_scale = 1.0 / z_total(turn)
        row_stage(turn, col_scale)

    def block_stats(offsets, piece):
        for slot, offset in enumerate(offsets):
            owner = lax.rem(z + offset, NZ)
            rows = pl.ds(pl.multiple_of(owner * BLOCK + piece * PIECE, PIECE), PIECE)
            weights[piece, slot * PIECE : (slot + 1) * PIECE, :] = (
                gibbs_t[rows, :].astype(F32) * row_scale[...]
            ).astype(BF16)
        return jnp.dot(
            weights[piece, 0 : len(offsets) * PIECE, :],
            lab_all[...],
            preferred_element_type=F32,
        )

    def stat_step(step):
        active = [c for c, (_, _, messages) in enumerate(CHAINS) if step < messages]
        away = [CHAINS[c][1] * (CHAINS[c][0] - step) % NZ for c in active]
        rest = []
        for piece in range(CHUNKS):
            partial = block_stats(away + [0] * (step == STEPS - 1), piece)
            for slot, chain in enumerate(active):
                _, way, messages = CHAINS[chain]
                device = at(dz=away[slot] if step == messages - 1 else way % NZ)
                value = partial[slot * PIECE : (slot + 1) * PIECE, :]
                if step:
                    arrived(
                        stat_land.at[chain, step - 1, piece],
                        s_stat.at[chain], r_stat.at[chain, step - 1, piece],
                    )
                    value = value + stat_land[chain, step - 1, piece]
                stat_src[chain, step, piece] = value
                send(
                    stat_src.at[chain, step, piece], stat_land.at[chain, step, piece],
                    s_stat.at[chain], r_stat.at[chain, step, piece], device,
                )
            rest.append(partial[len(active) * PIECE :, :])
        return rest

    stat_step(0)
    col_stage(ITERS)
    for d in range(1, QUAD):
        near = z // QUAD * QUAD + lax.rem(z + d, QUAD)
        send(z_src.at[ITERS], quad_land.at[d - 1], s_quad, r_quad, (y * NZ + near, cent))
    for wait in pending:
        wait()
    pending.clear()
    sent_later(quad_land, s_quad, r_quad)
    stat_step(1)
    arrived(quad_land, s_quad, r_quad)
    ring_src[...] = z_src[ITERS] + quad_land[0] + quad_land[1] + quad_land[2]
    for d in (2, 1, 3):
        send(ring_src, ring_land.at[d - 1], s_ring, r_ring, at(dz=d * QUAD))
    sent_later(ring_land, s_ring, r_ring)
    for step in range(2, STEPS):
        own = stat_step(step)
    for chain, (_, _, messages) in enumerate(CHAINS):
        sent_later(stat_src.at[chain, 0:messages], s_stat.at[chain], r_stat.at[chain, 0, 0])

    arrived(ring_land, s_ring, r_ring)
    mass = col_scale * (ring_src[...] + ring_land[0] + ring_land[1] + ring_land[2])
    mass_src[...] = mass
    for dy in Y_OFFSETS:
        send(mass_src, mass_land.at[dy - 1], s_mass, r_mass, at(dy=dy))
    sent_later(mass_land, s_mass, r_mass)
    mass_ref[y] = mass

    for piece in range(CHUNKS):
        part = slice(piece * PIECE, (piece + 1) * PIECE)
        stats = own[piece]
        for chain in reversed(range(len(CHAINS))):
            last = CHAINS[chain][2] - 1
            arrived(
                stat_land.at[chain, last, piece], s_stat.at[chain], r_stat.at[chain, last, piece]
            )
            stats = stats + stat_land[chain, last, piece]
        scale = lax.rsqrt(jnp.mean(stats * stats, axis=1, keepdims=True) + EPSILON)
        new_ref[part, :] = stats * scale

    arrived(mass_land, s_mass, r_mass)
    for dy in Y_OFFSETS:
        mass_ref[lax.rem(y + (NY - dy), NY)] = mass_land[dy - 1]

    for wait in pending:
        wait()


def shards(labels, counts, centroids):
    vmem = pl.BlockSpec(memory_space=pltpu.VMEM)
    dma = pltpu.SemaphoreType.DMA
    new, mass = pl.pallas_call(
        kernel,
        out_shape=(
            jax.ShapeDtypeStruct((BLOCK, FEAT), F32),
            jax.ShapeDtypeStruct((NY, 1, QUARTER), F32),
        ),
        in_specs=[
            pl.BlockSpec(memory_space=pltpu.SMEM),
            pl.BlockSpec(memory_space=pl.ANY),
            pl.BlockSpec(memory_space=pl.ANY),
        ],
        out_specs=(vmem, vmem),
        scratch_shapes=[
            pltpu.VMEM((LAB, FEAT), BF16),
            pltpu.VMEM((KC, FEAT), BF16),
            pltpu.VMEM((KC, FEAT), BF16),
            pltpu.VMEM((KC, LAB), BF16),
            pltpu.VMEM((QUARTER, WIDE), BF16),
            pltpu.VMEM((WIDE, FEAT), BF16),
            pltpu.VMEM((2, HALF + EXTRA, FEAT), F32),
            pltpu.VMEM((2, 2, HALF + EXTRA, FEAT), F32),
            pltpu.VMEM((1, WIDE), F32),
            pltpu.VMEM((1, WIDE), F32),
            pltpu.VMEM((CHUNKS, (len(CHAINS) + 1) * PIECE, WIDE), BF16),
            pltpu.VMEM((NY, 1, QUARTER), F32),
            pltpu.VMEM((NY - 1, 1, QUARTER), F32),
            pltpu.VMEM((SHARE, FEAT), F32),
            pltpu.VMEM((NX - 1, SHARE, FEAT), F32),
            pltpu.VMEM((NX, SHARE, FEAT), F32),
            pltpu.VMEM((2, EXTRA, FEAT), F32),
            pltpu.VMEM((ITERS + 1, 1, QUARTER), F32),
            pltpu.VMEM((ITERS, NZ - 1, 1, QUARTER), F32),
            pltpu.VMEM((ITERS, 2, 1, SIDE), F32),
            pltpu.VMEM((ITERS, 1, SIDE), F32),
            pltpu.VMEM((ITERS, 1, SIDE), F32),
            pltpu.VMEM((ITERS, NY * NX - 1, 1, SIDE), F32),
            pltpu.VMEM((ITERS, 1, SIDE), F32),
            pltpu.VMEM((ITERS, 1, SIDE), F32),
            pltpu.VMEM((QUAD - 1, 1, QUARTER), F32),
            pltpu.VMEM((1, QUARTER), F32),
            pltpu.VMEM((NZ // QUAD - 1, 1, QUARTER), F32),
            pltpu.VMEM((1, QUARTER), F32),
            pltpu.VMEM((NY - 1, 1, QUARTER), F32),
            pltpu.VMEM((len(CHAINS), STEPS, CHUNKS, PIECE, FEAT), F32),
            pltpu.VMEM((len(CHAINS), STEPS, CHUNKS, PIECE, FEAT), F32),
            dma((NY + 1,)),
            dma, dma,
            dma, dma((2,)),
            dma, dma((2,)),
            dma((ITERS,)), dma((ITERS,)),
            dma((ITERS,)), dma((ITERS,)),
            dma((ITERS,)), dma((ITERS,)),
            dma((ITERS,)), dma((ITERS,)),
            dma, dma,
            dma, dma,
            dma, dma,
            dma, dma,
            dma, dma,
            dma, dma,
            dma, dma,
            dma, dma,
            dma((len(CHAINS),)), dma((len(CHAINS), STEPS, CHUNKS)),
        ],
        compiler_params=pltpu.CompilerParams(
            collective_id=0, has_side_effects=True, vmem_limit_bytes=55040 << 10
        ),
        name="sinkhorn_assign",
    )(counts, labels, centroids)
    return new, mass.reshape(KC)


def solution(mesh):
    return jax.shard_map(
        shards,
        mesh=mesh,
        in_specs=(P("label", None), P("label"), P("cent", None)),
        out_specs=(P(("cent", "label"), None), P("cent")),
        check_vma=False,
    )
```

```python
import functools
import math

import jax
import jax.numpy as jnp
from jax import lax
from jax.experimental import pallas as pl
from jax.experimental.pallas import tpu as pltpu
from jax.sharding import PartitionSpec as P

ITERS = 3
SOFTMAX_HEAT = 0.02
EPSILON = 1e-06

F32, BF16 = jnp.float32, jnp.bfloat16
MESH = pl.DeviceIdType.MESH
NT = (((1,), (1,)), ((), ()))

NY, NZ, NX, NK = 4, 16, 4, 2
LAB = 512
HALF = LAB // 2
WIDE = NY * LAB
KC = 4096
QUARTER = KC // NY
SIDE = WIDE // 2
FEAT = 256
BLOCK = QUARTER // NZ
TILE = 256
EXTRA = 8
CHUNKS = 2
CHAINS = ((8, 1, 4), (7, -1, 4), (4, 1, 4), (3, -1, 3))
STEPS = max(messages for _, _, messages in CHAINS)
PIECE = BLOCK // CHUNKS
QUAD = 4
SHARE = HALF // NX


def distance(offset, size):
    return min(offset, size - offset)


Y_OFFSETS = (2, 1, 3)
PART_ORDER = (2, 1, 3, 0)
Z_OFFSETS = sorted(range(1, NZ), key=lambda d: -distance(d, NZ))
XY_OFFSETS = sorted(
    [(dy, dx) for dy in range(NY) for dx in range(NX) if dy or dx],
    key=lambda o: -(distance(o[0], NY) + distance(o[1], NX)),
)


X_OFFSETS = (2, 1, 3)


def unit(values):
    wide = values.astype(F32)
    scale = lax.rsqrt(jnp.mean(wide * wide, axis=1, keepdims=True) + EPSILON)
    return (wide * scale).astype(BF16)


def gibbs(centroid_unit, label_unit):
    scores = lax.dot_general(centroid_unit, label_unit, NT, preferred_element_type=F32)
    return jnp.exp2(scores * (math.log2(math.e) / (SOFTMAX_HEAT * FEAT))).astype(BF16)


def split_rows(vector):
    high = vector.astype(BF16).astype(F32)
    rest = vector - high
    row = lax.broadcasted_iota(jnp.int32, (16, vector.shape[1]), 0)
    return jnp.where(row == 0, high, jnp.where(row == 1, rest, 0.0)).astype(BF16)


def joined(rows):
    return rows[0:1, :] + rows[1:2, :]


def kernel(
    counts_ref,
    lab_hbm,
    cen_hbm,
    new_ref,
    mass_ref,
    lab_ref,
    cen_ref,
    cen_unit,
    wide_gibbs,
    gibbs_t,
    lab_all,
    lab_send,
    lab_land,
    mask_all,
    row_scale,
    weights,
    first_src,
    first_land,
    far_land,
    far_x,
    far_core,
    far_mask,
    z_src,
    z_land,
    core_src,
    core_land,
    xy_src,
    xy_land,
    half_src,
    half_land,
    quad_land,
    ring_src,
    ring_land,
    mass_src,
    mass_land,
    stat_src,
    stat_land,
    in_sem,
    s_first, r_first,
    s_lab, r_lab,
    s_fwd, r_fwd,
    s_z, r_z,
    s_core, r_core,
    s_xy, r_xy,
    s_half, r_half,
    s_quad, r_quad,
    s_ring, r_ring,
    s_mass, r_mass,
    s_far, r_far,
    s_far_x, r_far_x,
    s_far_core, r_far_core,
    s_far_rest, r_far_rest,
    s_far_mask, r_far_mask,
    s_stat, r_stat,
):
    label, cent = lax.axis_index("label"), lax.axis_index("cent")
    y, z = label // NZ, lax.rem(label, NZ)
    x, k = cent // NK, lax.rem(cent, NK)
    other = 1 - k

    copies = [pltpu.make_async_copy(lab_hbm, lab_ref, in_sem.at[NY])]
    for dy in PART_ORDER:
        rows = pl.ds(pl.multiple_of(lax.rem(y + dy, NY) * QUARTER, QUARTER), QUARTER)
        copies.append(
            pltpu.make_async_copy(cen_hbm.at[rows, :], cen_ref.at[rows, :], in_sem.at[dy])
        )
    for copy in copies:
        copy.start()

    def at(dy=0, dz=0, dx=0):
        return (
            lax.rem(y + dy, NY) * NZ + lax.rem(z + dz, NZ),
            lax.rem(x + dx, NX) * NK + k,
        )

    partner = (label, x * NK + other)

    def send(src, dst, send_sem, recv_sem, device):
        pltpu.make_async_remote_copy(
            src_ref=src,
            dst_ref=dst,
            send_sem=send_sem,
            recv_sem=recv_sem,
            device_id=device,
            device_id_type=MESH,
        ).start()

    def arrived(dst, send_sem, recv_sem):
        pltpu.make_async_remote_copy(
            src_ref=dst,
            dst_ref=dst,
            send_sem=send_sem,
            recv_sem=recv_sem,
            device_id=partner,
            device_id_type=MESH,
        ).wait_recv()

    def sent(src, send_sem, recv_sem):
        pltpu.make_async_remote_copy(
            src_ref=src,
            dst_ref=src,
            send_sem=send_sem,
            recv_sem=recv_sem,
            device_id=partner,
            device_id_type=MESH,
        ).wait_send()

    pending = []

    def sent_later(src, send_sem, recv_sem):
        pending.append(functools.partial(sent, src, send_sem, recv_sem))

    barrier = pltpu.get_barrier_semaphore()
    for dz in Z_OFFSETS:
        pl.semaphore_signal(barrier, inc=1, device_id=at(dz=dz), device_id_type=MESH)
    for dy, dx in XY_OFFSETS:
        pl.semaphore_signal(
            barrier, inc=1, device_id=at(dy=dy, dx=dx), device_id_type=MESH
        )
    pl.semaphore_signal(barrier, inc=1, device_id=partner, device_id_type=MESH)

    count = counts_ref[0]
    copies[0].wait()
    own_rows = pl.multiple_of(y * LAB, LAB)
    for half in range(2):
        rows = slice(half * HALF, (half + 1) * HALF)
        unit_half = unit(lab_ref[rows, :])
        lab_all[pl.ds(own_rows + half * HALF, HALF), :] = unit_half
        lab_send[half, 0:HALF, :] = unit_half.astype(F32)
        slot = lax.broadcasted_iota(jnp.int32, (EXTRA, HALF), 1) + half * HALF
        lab_send[half, HALF : HALF + EXTRA, :] = jnp.where(slot < count, 1.0, 0.0)
    slot = lax.broadcasted_iota(jnp.int32, (16, LAB), 1)
    own_mask = jnp.where(slot < count, 1.0, 0.0)
    mask_all[:, pl.ds(own_rows, LAB)] = own_mask[0:1, :]
    own_unit = lab_all[pl.ds(own_rows, LAB), :]

    scale_rows = split_rows(own_mask[0:1, :])

    def first_part(dy):
        part = lax.rem(y + dy, NY)
        copies[1 + PART_ORDER.index(dy)].wait()
        for j in range(QUARTER // TILE):
            rows = pl.ds(pl.multiple_of(part * QUARTER + j * TILE, TILE), TILE)
            tile_unit = unit(cen_ref[rows, :])
            cen_unit[rows, :] = tile_unit
            tile = gibbs(tile_unit, own_unit)
            wide_gibbs[rows, :] = tile
            if dy == 0:
                gibbs_t[j * TILE : (j + 1) * TILE, pl.ds(own_rows, LAB)] = tile
            sums = lax.dot_general(scale_rows, tile, NT, preferred_element_type=F32)
            first_src[part, :, j * TILE : (j + 1) * TILE] = joined(sums)

    for dy in Y_OFFSETS:
        first_part(dy)
    pl.semaphore_wait(barrier, NZ - 1 + NY * NX - 1 + 1)

    def lab_exchange(dy):
        send(
            lab_send.at[k], lab_land.at[dy // 2, k],
            s_lab, r_lab.at[dy // 2], at(dy=dy),
        )

    for dy in Y_OFFSETS:
        send(
            first_src.at[lax.rem(y + dy, NY)], first_land.at[dy - 1],
            s_first, r_first, at(dy=dy),
        )
    send(
        lab_send.at[k, pl.ds(pl.multiple_of(x * SHARE, SHARE), SHARE), :], far_land,
        s_far, r_far, at(dy=2),
    )
    send(lab_send.at[:, HALF : HALF + EXTRA, :], far_mask, s_far_mask, r_far_mask, at(dy=2))
    for dy in (1, 3):
        lab_exchange(dy)
    first_part(0)
    sent_later(first_land, s_first, r_first)
    sent_later(far_land, s_far, r_far)
    sent_later(far_mask, s_far_mask, r_far_mask)
    sent_later(lab_land.at[:, k], s_lab, r_lab.at[0])

    def z_send(turn):
        for dz in Z_OFFSETS:
            send(z_src.at[turn], z_land.at[turn, dz - 1], s_z.at[turn], r_z.at[turn], at(dz=dz))
        sent_later(z_land.at[turn], s_z.at[turn], r_z.at[turn])

    def z_total(turn):
        arrived(z_land.at[turn], s_z.at[turn], r_z.at[turn])
        total = z_src[turn]
        for slot in range(NZ - 1):
            total = total + z_land[turn, slot]
        return total

    arrived(first_land, s_first, r_first)
    z_src[0] = first_src[y] + first_land[0] + first_land[1] + first_land[2]
    z_send(0)

    arrived(far_land, s_far, r_far)
    for dx in X_OFFSETS:
        send(far_land, far_x.at[dx - 1], s_far_x, r_far_x, at(dx=dx))
    send(far_land, far_core.at[0], s_far_core, r_far_core, partner)
    sent_later(far_x, s_far_x, r_far_x)
    sent_later(far_land, s_far_core, r_far_core)

    def fill(owner, half):
        rows = pl.ds(pl.multiple_of(owner * LAB + half * HALF, HALF), HALF)
        for j in range(QUARTER // TILE):
            mine = pl.ds(pl.multiple_of(y * QUARTER + j * TILE, TILE), TILE)
            gibbs_t[j * TILE : (j + 1) * TILE, rows] = gibbs(cen_unit[mine, :], lab_all[rows, :])

    def take(dy, half):
        owner = lax.rem(y + (NY - dy), NY)
        rows = pl.ds(pl.multiple_of(owner * LAB + half * HALF, HALF), HALF)
        lab_all[rows, :] = lab_land[dy // 2, half, 0:HALF, :].astype(BF16)
        mask_all[:, rows] = lab_land[dy // 2, half, HALF : HALF + 1, :]
        fill(owner, half)

    def take_far(half, quarters):
        owner = lax.rem(y + 2, NY)
        start = owner * LAB + half * HALF
        for dx, quarter in enumerate(quarters):
            first = start + lax.rem(x + (NX - dx), NX) * SHARE
            lab_all[pl.ds(pl.multiple_of(first, SHARE), SHARE), :] = quarter[...].astype(BF16)
        mask_all[:, pl.ds(pl.multiple_of(start, HALF), HALF)] = far_mask[half, 0:1, :]
        fill(owner, half)

    def hand_over(dy):
        arrived(lab_land.at[dy // 2, k], s_lab, r_lab.at[dy // 2])
        send(
            lab_land.at[dy // 2, k], lab_land.at[dy // 2, k],
            s_fwd, r_fwd.at[dy // 2], partner,
        )

    def other_after(dy):
        arrived(lab_land.at[dy // 2, other], s_fwd, r_fwd.at[dy // 2])
        return other

    for dy in (1, 3):
        hand_over(dy)
    arrived(far_x, s_far_x, r_far_x)
    send(far_x, far_core.at[1:NX], s_far_rest, r_far_rest, partner)
    sent_later(lab_land.at[:, k], s_fwd, r_fwd.at[0])
    sent_later(far_x, s_far_rest, r_far_rest)
    take(1, k)
    take(3, k)
    arrived(far_mask, s_far_mask, r_far_mask)
    take_far(k, [far_land] + [far_x.at[dx - 1] for dx in range(1, NX)])
    for dy in (1, 3):
        take(dy, other_after(dy))
    arrived(far_core.at[0], s_far_core, r_far_core)
    arrived(far_core.at[1:NX], s_far_rest, r_far_rest)
    take_far(other, [far_core.at[dx] for dx in range(NX)])

    def row_stage(turn, col_scale):
        scale_rows = split_rows(col_scale)
        def half_sums(half):
            columns = pl.ds(pl.multiple_of(half * SIDE, SIDE), SIDE)
            core_src[turn, half] = joined(
                jnp.dot(scale_rows, gibbs_t[:, columns], preferred_element_type=F32)
            )

        half_sums(other)
        send(core_src.at[turn, other], core_land.at[turn], s_core.at[turn], r_core.at[turn], partner)
        half_sums(k)
        sent_later(core_land.at[turn], s_core.at[turn], r_core.at[turn])
        arrived(core_land.at[turn], s_core.at[turn], r_core.at[turn])
        xy_src[turn] = core_src[turn, k] + core_land[turn]
        for dy, dx in XY_OFFSETS:
            send(
                xy_src.at[turn], xy_land.at[turn, dy * NX + dx - 1],
                s_xy.at[turn], r_xy.at[turn], at(dy=dy, dx=dx),
            )
        sent_later(xy_land.at[turn], s_xy.at[turn], r_xy.at[turn])
        arrived(xy_land.at[turn], s_xy.at[turn], r_xy.at[turn])
        total = xy_src[turn]
        for slot in range(NY * NX - 1):
            total = total + xy_land[turn, slot]
        mine = pl.ds(pl.multiple_of(k * SIDE, SIDE), SIDE)
        scale = mask_all[:, mine] / total
        half_src[turn] = scale
        send(half_src.at[turn], half_land.at[turn], s_half.at[turn], r_half.at[turn], partner)
        sent_later(half_land.at[turn], s_half.at[turn], r_half.at[turn])
        row_scale[:, mine] = scale
        mine_sums = col_sums(scale, k)
        arrived(half_land.at[turn], s_half.at[turn], r_half.at[turn])
        row_scale[:, pl.ds(pl.multiple_of(other * SIDE, SIDE), SIDE)] = half_land[turn]
        return mine_sums

    def col_sums(scale, half):
        columns = pl.ds(pl.multiple_of(half * SIDE, SIDE), SIDE)
        return joined(
            lax.dot_general(
                split_rows(scale), gibbs_t[:, columns], NT, preferred_element_type=F32
            )
        )

    def col_stage(turn, mine_sums):
        z_src[turn] = mine_sums + col_sums(half_land[turn - 1], other)

    col_scale = 1.0 / z_total(0)
    for turn in range(ITERS):
        if turn:
            col_stage(turn, mine_sums)
            z_send(turn)
            col_scale = 1.0 / z_total(turn)
        mine_sums = row_stage(turn, col_scale)

    def block_stats(offsets, piece):
        for slot, offset in enumerate(offsets):
            owner = lax.rem(z + offset, NZ)
            rows = pl.ds(pl.multiple_of(owner * BLOCK + piece * PIECE, PIECE), PIECE)
            weights[piece, slot * PIECE : (slot + 1) * PIECE, :] = (
                gibbs_t[rows, :].astype(F32) * row_scale[...]
            ).astype(BF16)
        return jnp.dot(
            weights[piece, 0 : len(offsets) * PIECE, :],
            lab_all[...],
            preferred_element_type=F32,
        )

    def stat_step(step):
        active = [c for c, (_, _, messages) in enumerate(CHAINS) if step < messages]
        away = [CHAINS[c][1] * (CHAINS[c][0] - step) % NZ for c in active]
        rest = []
        for piece in range(CHUNKS):
            partial = block_stats(away + [0] * (step == STEPS - 1), piece)
            for slot, chain in enumerate(active):
                _, way, messages = CHAINS[chain]
                device = at(dz=away[slot] if step == messages - 1 else way % NZ)
                value = partial[slot * PIECE : (slot + 1) * PIECE, :]
                if step:
                    arrived(
                        stat_land.at[chain, step - 1, piece],
                        s_stat.at[chain], r_stat.at[chain, step - 1, piece],
                    )
                    value = value + stat_land[chain, step - 1, piece]
                stat_src[chain, step, piece] = value
                send(
                    stat_src.at[chain, step, piece], stat_land.at[chain, step, piece],
                    s_stat.at[chain], r_stat.at[chain, step, piece], device,
                )
            rest.append(partial[len(active) * PIECE :, :])
        return rest

    stat_step(0)
    col_stage(ITERS, mine_sums)
    for d in range(1, QUAD):
        near = z // QUAD * QUAD + lax.rem(z + d, QUAD)
        send(z_src.at[ITERS], quad_land.at[d - 1], s_quad, r_quad, (y * NZ + near, cent))
    for wait in pending:
        wait()
    pending.clear()
    sent_later(quad_land, s_quad, r_quad)
    stat_step(1)
    arrived(quad_land, s_quad, r_quad)
    ring_src[...] = z_src[ITERS] + quad_land[0] + quad_land[1] + quad_land[2]
    for d in (2, 1, 3):
        send(ring_src, ring_land.at[d - 1], s_ring, r_ring, at(dz=d * QUAD))
    sent_later(ring_land, s_ring, r_ring)
    for step in range(2, STEPS):
        own = stat_step(step)
    for chain, (_, _, messages) in enumerate(CHAINS):
        sent_later(stat_src.at[chain, 0:messages], s_stat.at[chain], r_stat.at[chain, 0, 0])

    arrived(ring_land, s_ring, r_ring)
    mass = col_scale * (ring_src[...] + ring_land[0] + ring_land[1] + ring_land[2])
    mass_src[...] = mass
    for dy in Y_OFFSETS:
        send(mass_src, mass_land.at[dy - 1], s_mass, r_mass, at(dy=dy))
    sent_later(mass_land, s_mass, r_mass)
    mass_ref[y] = mass

    for piece in range(CHUNKS):
        part = slice(piece * PIECE, (piece + 1) * PIECE)
        stats = own[piece]
        for chain in reversed(range(len(CHAINS))):
            last = CHAINS[chain][2] - 1
            arrived(
                stat_land.at[chain, last, piece], s_stat.at[chain], r_stat.at[chain, last, piece]
            )
            stats = stats + stat_land[chain, last, piece]
        scale = lax.rsqrt(jnp.mean(stats * stats, axis=1, keepdims=True) + EPSILON)
        new_ref[part, :] = stats * scale

    arrived(mass_land, s_mass, r_mass)
    for dy in Y_OFFSETS:
        mass_ref[lax.rem(y + (NY - dy), NY)] = mass_land[dy - 1]

    for wait in pending:
        wait()


def shards(labels, counts, centroids):
    vmem = pl.BlockSpec(memory_space=pltpu.VMEM)
    dma = pltpu.SemaphoreType.DMA
    new, mass = pl.pallas_call(
        kernel,
        out_shape=(
            jax.ShapeDtypeStruct((BLOCK, FEAT), F32),
            jax.ShapeDtypeStruct((NY, 1, QUARTER), F32),
        ),
        in_specs=[
            pl.BlockSpec(memory_space=pltpu.SMEM),
            pl.BlockSpec(memory_space=pl.ANY),
            pl.BlockSpec(memory_space=pl.ANY),
        ],
        out_specs=(vmem, vmem),
        scratch_shapes=[
            pltpu.VMEM((LAB, FEAT), BF16),
            pltpu.VMEM((KC, FEAT), BF16),
            pltpu.VMEM((KC, FEAT), BF16),
            pltpu.VMEM((KC, LAB), BF16),
            pltpu.VMEM((QUARTER, WIDE), BF16),
            pltpu.VMEM((WIDE, FEAT), BF16),
            pltpu.VMEM((2, HALF + EXTRA, FEAT), F32),
            pltpu.VMEM((2, 2, HALF + EXTRA, FEAT), F32),
            pltpu.VMEM((1, WIDE), F32),
            pltpu.VMEM((1, WIDE), F32),
            pltpu.VMEM((CHUNKS, (len(CHAINS) + 1) * PIECE, WIDE), BF16),
            pltpu.VMEM((NY, 1, QUARTER), F32),
            pltpu.VMEM((NY - 1, 1, QUARTER), F32),
            pltpu.VMEM((SHARE, FEAT), F32),
            pltpu.VMEM((NX - 1, SHARE, FEAT), F32),
            pltpu.VMEM((NX, SHARE, FEAT), F32),
            pltpu.VMEM((2, EXTRA, FEAT), F32),
            pltpu.VMEM((ITERS + 1, 1, QUARTER), F32),
            pltpu.VMEM((ITERS, NZ - 1, 1, QUARTER), F32),
            pltpu.VMEM((ITERS, 2, 1, SIDE), F32),
            pltpu.VMEM((ITERS, 1, SIDE), F32),
            pltpu.VMEM((ITERS, 1, SIDE), F32),
            pltpu.VMEM((ITERS, NY * NX - 1, 1, SIDE), F32),
            pltpu.VMEM((ITERS, 1, SIDE), F32),
            pltpu.VMEM((ITERS, 1, SIDE), F32),
            pltpu.VMEM((QUAD - 1, 1, QUARTER), F32),
            pltpu.VMEM((1, QUARTER), F32),
            pltpu.VMEM((NZ // QUAD - 1, 1, QUARTER), F32),
            pltpu.VMEM((1, QUARTER), F32),
            pltpu.VMEM((NY - 1, 1, QUARTER), F32),
            pltpu.VMEM((len(CHAINS), STEPS, CHUNKS, PIECE, FEAT), F32),
            pltpu.VMEM((len(CHAINS), STEPS, CHUNKS, PIECE, FEAT), F32),
            dma((NY + 1,)),
            dma, dma,
            dma, dma((2,)),
            dma, dma((2,)),
            dma((ITERS,)), dma((ITERS,)),
            dma((ITERS,)), dma((ITERS,)),
            dma((ITERS,)), dma((ITERS,)),
            dma((ITERS,)), dma((ITERS,)),
            dma, dma,
            dma, dma,
            dma, dma,
            dma, dma,
            dma, dma,
            dma, dma,
            dma, dma,
            dma, dma,
            dma((len(CHAINS),)), dma((len(CHAINS), STEPS, CHUNKS)),
        ],
        compiler_params=pltpu.CompilerParams(
            collective_id=0, has_side_effects=True, vmem_limit_bytes=55040 << 10
        ),
        name="sinkhorn_assign",
    )(counts, labels, centroids)
    return new, mass.reshape(KC)


def solution(mesh):
    return jax.shard_map(
        shards,
        mesh=mesh,
        in_specs=(P("label", None), P("label"), P("cent", None)),
        out_specs=(P(("cent", "label"), None), P("cent")),
        check_vma=False,
    )
```
